32 devices in a mesh: feed: 4 (over y, x), freq: 8 (over z, core).
Axes of the slice: x: 2, y: 2, z: 4, core: 2. Of those that a mesh axis runs over, the one named last changes fastest.
Arguments:
- voltage: bfloat16 [2, 1024, 32768], P(None, 'feed', 'freq'), may hold values from -6 to 6
- flags: int32 [4, 128], P('feed'), may hold values 0 or 1
- owner_slot: int32 [128], replicated, may hold values from 0 to 159, as said below
Outputs:
- visibility: bfloat16 [160, 2, 1024, 1024], P('freq', None, 'feed')
The draws below stay inside these ranges and needn't reach their ends.
Inputs may be any that keep to these rules, and one draw needn't show every extreme that they name: `owner_slot`: distinct slots; slot s belongs to owner s // 20 of freq. No owner gets more than 20 channels, and some owner gets exactly 20.
All inputs are finite; a program needn't handle non-finite values. No bound on the sum of `flags` on one device may be relied on, other than what follows from the above.
Results may differ from the reference program's by a relative error of at most 0.0073.
Values may be sent and summed in bfloat16 or wider, within the bound.
A program may use at most 192 MiB of HBM per device.

```python
import math
import jax
import jax.numpy as jnp
from jax import lax

F = 1024
CH = 1024
TAPS = 4
BAND_LO = 256
CAP = 20
BAND = 128
NSPEC = 32
SAMPLES = 32768
N_FEED = 4
N_FREQ = 8


def draw_owner_slot(key, part):
    key = jax.random.fold_in(key, 7)
    first, second, third = jax.random.split(key, 3)
    slot_count = N_FREQ * CAP
    filled = jax.random.randint(first, (), 0, N_FREQ)
    scores = jax.random.permutation(second, slot_count).astype(jnp.int32)
    slot_ids = jnp.arange(slot_count, dtype=jnp.int32)
    scores = jnp.where(slot_ids // CAP == filled, slot_ids - slot_count, scores)
    ordered = jnp.argsort(scores, stable=True)
    chosen = ordered[:BAND]
    return jax.random.permutation(third, chosen).astype(jnp.int32)


def touch_ends(entries, rng, smallest, high):
    extent = entries.shape
    spot = [jax.random.randint(jax.random.fold_in(rng, axis), (), 0, extent[axis]) for axis in range(len(extent))]
    entries = entries.at[tuple(spot)].set(smallest)
    longest = extent.index(max(extent))
    spot[longest] = (spot[longest] + 1) % extent[longest]
    return entries.at[tuple(spot)].set(high)


def block_scale(stream_key, dims, shards, low, largest):
    gain = 1.0
    for dim, shards_of in shards:
        heights = jax.random.uniform(jax.random.fold_in(jax.random.fold_in(stream_key, 6), dim), (shards_of,), jnp.float32, low / len(shards), largest / len(shards))
        gain = gain * jnp.repeat(jnp.exp(heights), dims[dim] // shards_of).reshape((-1,) + (1,) * (len(dims) - 1 - dim))
    return gain


def normal_values(key, shape, deviation, bound, pieces=(), kind=jnp.bfloat16):
    drawn = deviation * jax.random.normal(key, shape, jnp.float32)
    if pieces:
        drawn = drawn * block_scale(key, shape, pieces, -0.22, 0.18)
    return jnp.clip(drawn, -bound, bound).astype(kind)


def setup_inputs(seed: int = 0) -> dict:
    seeds = jax.random.split(jax.random.key(seed), 4)
    return {
        "voltage": normal_values(seeds[0], (2, F, SAMPLES), 1.0, 6.0, ((1, 4), (2, 8))),
        "flags": touch_ends((jax.random.randint(seeds[1], (N_FEED, BAND), 0, 4) < 3).astype(jnp.int32), jax.random.fold_in(seeds[1], 1), 0, 1),
        "owner_slot": draw_owner_slot(jax.random.fold_in(seeds[3], 71), 0),
    }


def prototype():
    total = TAPS * CH
    position = jnp.arange(total, dtype=jnp.int32).astype(jnp.float32)
    offset = (position - total / 2 + 0.5) / CH
    taper = 0.5 - 0.5 * jnp.cos(2 * jnp.pi * (position + 0.5) / total)
    coeffs = jnp.sinc(offset) * taper
    coeffs = coeffs * jnp.sqrt(CH / jnp.sum(coeffs * coeffs))
    return coeffs.reshape(TAPS, CH)

def tables(band):
    sample = jnp.arange(CH, dtype=jnp.int32)
    channel = jnp.arange(band, dtype=jnp.int32) + BAND_LO
    phase = (sample[:, None] * channel[None, :] % CH).astype(jnp.float32) * (2 * jnp.pi / CH)
    return (jnp.cos(phase).astype(jnp.bfloat16), jnp.sin(phase).astype(jnp.bfloat16))

def channelize(voltage, extra, flag_row):
    band = flag_row.shape[0]
    longer = jnp.concatenate([voltage, extra], 2)
    count = voltage.shape[2] // CH
    feeds = voltage.shape[1]
    blocks = longer.reshape(2, feeds, count + TAPS - 1, CH)
    coeffs = prototype()
    summed = blocks[:, :, 0:count, :].astype(jnp.float32) * coeffs[0]
    for tap_index in range(1, TAPS):
        summed = summed + blocks[:, :, tap_index:tap_index + count, :].astype(jnp.float32) * coeffs[tap_index]
    weighted = summed.astype(jnp.bfloat16)
    cosine, sine = tables(band)
    real_rows = weighted[0].reshape(feeds * count, CH)
    imag_rows = weighted[1].reshape(feeds * count, CH)
    real_part = jnp.dot(real_rows, cosine, preferred_element_type=jnp.float32) + jnp.dot(imag_rows, sine, preferred_element_type=jnp.float32)
    imag_part = jnp.dot(imag_rows, cosine, preferred_element_type=jnp.float32) - jnp.dot(real_rows, sine, preferred_element_type=jnp.float32)
    joined = jnp.stack([real_part, imag_part], 0).reshape(2, feeds, count, band)
    joined = joined * (flag_row.astype(jnp.float32) * (1.0 / math.sqrt(CH)))
    return jnp.transpose(joined, (3, 0, 2, 1)).astype(jnp.bfloat16)

def reference(voltage, flags, owner_slot):
    group_feeds = F // N_FEED
    groups = jnp.transpose(voltage.reshape(2, N_FEED, group_feeds, SAMPLES), (1, 0, 2, 3))
    padding = jnp.zeros((N_FEED, 2, group_feeds, (TAPS - 1) * CH), jnp.bfloat16)

    def one_group(bundle):
        return channelize(bundle[0], bundle[1], bundle[2])
    spectra = lax.map(one_group, (groups, padding, flags))
    spectra = jnp.transpose(spectra, (1, 2, 3, 0, 4)).reshape(BAND, 2, NSPEC, F)
    inverse = 1.0 / NSPEC

    def correlate(block):
        wide = block.astype(jnp.float32)
        swapped = jnp.stack([wide[1], -wide[0]], 0)
        real_vis = jnp.einsum('zsf,zsg->fg', wide, wide, precision=lax.Precision.HIGHEST)
        imag_vis = jnp.einsum('zsf,zsg->fg', wide, swapped, precision=lax.Precision.HIGHEST)
        return (jnp.stack([real_vis, imag_vis], 0) * inverse).astype(jnp.bfloat16)
    visible = lax.map(correlate, spectra)
    result = jnp.zeros((N_FREQ * CAP, 2, F, F), jnp.bfloat16)
    return result.at[owner_slot].set(visible)
```

```python
import functools
import math

import jax
import jax.numpy as jnp
import ml_dtypes
import numpy as np
from jax import lax
from jax.experimental import pallas as pl
from jax.experimental.pallas import tpu as pltpu
from jax.sharding import PartitionSpec as P

CH = 1024
TAPS = 4
BAND_LO = 256
CAP = 20
QUAD = 4
GROUPS = CAP // QUAD
MESH = pl.DeviceIdType.MESH
MIB = 1024 * 1024


def prototype():
    total = TAPS * CH
    position = np.arange(total, dtype=np.float64)
    taper = 0.5 - 0.5 * np.cos(2 * np.pi * (position + 0.5) / total)
    coeffs = np.sinc((position - total / 2 + 0.5) / CH) * taper
    coeffs = coeffs * np.sqrt(CH / np.sum(coeffs * coeffs))
    return coeffs.reshape(TAPS, CH).astype(np.float32)


def tables(band):
    phase = (np.arange(band)[:, None] + BAND_LO) * np.arange(CH)[None, :] % CH * (2 * np.pi / CH)
    cosine = np.cos(phase).astype(np.float32).astype(ml_dtypes.bfloat16)
    sine = np.sin(phase).astype(np.float32).astype(ml_dtypes.bfloat16)
    return np.concatenate(
        [np.concatenate([cosine, sine], 1), np.concatenate([-sine, cosine], 1)], 0
    )


def spread_kernel(
    count, owners, voltage, coeffs, table, flags, owner_slot, gathered,
    slot_table, weighted, halo_out, halo_in, parts, outgoing,
    halo_send, halo_recv, local_sem, a_send, a_recv, x_send, x_recv, y_send, y_recv, d_send, d_recv,
):
    feed, me = lax.axis_index("feed"), lax.axis_index("freq")
    feeds = voltage.shape[1]
    band = flags.shape[1]
    rows = slot_table.shape[0]
    along_x, along_y = feed ^ 1, feed ^ 2

    barrier = pltpu.get_barrier_semaphore()
    for step in range(1, owners):
        pl.semaphore_signal(barrier, inc=1, device_id=(feed, me ^ step), device_id_type=MESH)
    for other in (along_x, along_y):
        pl.semaphore_signal(barrier, inc=1, device_id=(other, me), device_id_type=MESH)

    row = lax.broadcasted_iota(jnp.int32, (rows, band), 0)
    slot = row // (2 * QUAD) * QUAD + row % QUAD
    kept = jnp.where(slot == owner_slot[...], flags[...].astype(jnp.float32), 0.0)
    kept = kept * (1.0 / math.sqrt(CH))
    imag_row = row // QUAD % 2 == 1
    slot_table[...] = (
        jnp.dot(
            jnp.where(imag_row, 0.0, kept).astype(jnp.bfloat16),
            table[0:band, :],
            preferred_element_type=jnp.float32,
        )
        + jnp.dot(
            jnp.where(imag_row, kept, 0.0).astype(jnp.bfloat16),
            table[band : 2 * band, :],
            preferred_element_type=jnp.float32,
        )
    ).astype(jnp.bfloat16)

    def weigh(sums):
        tall = 32

        @pl.loop(0, feeds // tall)
        def _(index):
            here = pl.ds(pl.multiple_of(index * tall, tall), tall)
            for part in range(2):
                for lane in range(0, CH, 128):
                    blocks = [
                        voltage[part, here, block * CH + lane : block * CH + lane + 128].astype(jnp.float32)
                        for block in range(count)
                    ]
                    for place, pairs in enumerate(sums):
                        total = None
                        for tap, block in pairs:
                            term = blocks[block] * coeffs[tap : tap + 1, lane : lane + 128]
                            total = term if total is None else total + term
                        weighted[place, here, part * CH + lane : part * CH + lane + 128] = total.astype(
                            jnp.bfloat16
                        )

    def transform(place):
        return lax.dot_general(
            slot_table[...],
            weighted[place],
            (((1,), (1,)), ((), ())),
            preferred_element_type=jnp.float32,
        )

    halo = TAPS - 1
    weigh(
        [
            [(tap, spectrum + tap - count) for tap in range(TAPS) if 0 <= spectrum + tap - count < count]
            for spectrum in range(count - halo, count)
        ]
    )

    @pl.loop(0, halo)
    def _(place):
        halo_out[place] = transform(place).astype(jnp.bfloat16)

    pl.semaphore_wait(barrier, owners + 1)
    backward = pltpu.make_async_remote_copy(
        src_ref=halo_out,
        dst_ref=halo_in,
        send_sem=halo_send,
        recv_sem=halo_recv,
        device_id=(feed, jnp.maximum(me - 1, 0)),
        device_id_type=MESH,
    )

    @pl.when(me > 0)
    def _():
        backward.start()

    weigh(
        [
            [(tap, spectrum + tap) for tap in range(TAPS) if spectrum + tap < count]
            for spectrum in range(count)
        ]
    )

    @pl.loop(0, count)
    def _(place):
        parts[place] = transform(place)

    @pl.when(me < owners - 1)
    def _():
        backward.wait_recv()
        for place in range(halo):
            parts[count - halo + place] += halo_in[place].astype(jnp.float32)

    for place in range(0, count, 2):
        pair = [parts[place + k].reshape(rows // 8, 8, feeds) for k in range(2)]
        outgoing[:, place * 8 : place * 8 + 16, :] = jnp.concatenate(pair, 1).astype(jnp.bfloat16)

    def chunk(owner):
        return outgoing.at[pl.ds(owner * GROUPS, GROUPS)]

    keep = pltpu.make_async_copy(chunk(me), gathered.at[feed, me], local_sem)
    keep.start()

    def remote(source, target, send, recv, device):
        return pltpu.make_async_remote_copy(
            src_ref=source, dst_ref=target, send_sem=send, recv_sem=recv, device_id=device, device_id_type=MESH
        )

    to_owner = [None] + [
        remote(chunk(me ^ t), gathered.at[feed, me], a_send.at[t], a_recv.at[t], (feed, me ^ t))
        for t in range(1, owners)
    ]

    def shared(t):
        return chunk(me) if t == 0 else gathered.at[feed, me ^ t]

    to_x = [
        remote(shared(t), gathered.at[feed, me ^ t], x_send.at[t], x_recv.at[t], (along_x, me))
        for t in range(owners)
    ]
    to_y = [
        remote(shared(t), gathered.at[feed, me ^ t], y_send.at[t], y_recv.at[t], (along_y, me))
        for t in range(owners)
    ]
    onward = []
    for t in range(owners):
        origin, target = (along_x, along_y) if t % 2 else (along_y, along_x)
        block = gathered.at[origin, me ^ t]
        onward.append(remote(block, block, d_send.at[t], d_recv.at[t], (target, me)))

    def pass_on(t):
        (to_x if t % 2 else to_y)[t].wait_recv()
        onward[t].start()

    to_x[0].start()
    to_y[0].start()
    for t in range(1, owners):
        to_owner[t].start()
    for t in range(1, owners):
        to_owner[t].wait_recv()
        to_x[t].start()
        to_y[t].start()
        pass_on(t - 1)
    pass_on(owners - 1)

    keep.wait()
    for t in range(owners):
        (to_y if t % 2 else to_x)[t].wait_recv()
        onward[t].wait_recv()
        if t:
            to_owner[t].wait_send()
        to_x[t].wait_send()
        to_y[t].wait_send()
        onward[t].wait_send()

    @pl.when(me > 0)
    def _():
        backward.wait_send()


def spread(voltage, flags, owner_slot, feed_groups, owners):
    feeds, samples = voltage.shape[1:]
    band = flags.shape[1]
    count = samples // CH
    rows = owners * CAP * 2
    tall = count * 2 * QUAD
    vmem = pl.BlockSpec(memory_space=pltpu.VMEM)
    dma = pltpu.SemaphoreType.DMA
    return pl.pallas_call(
        functools.partial(spread_kernel, count, owners),
        out_shape=jax.ShapeDtypeStruct((feed_groups, owners, GROUPS, tall, feeds), jnp.bfloat16),
        in_specs=[vmem] * 5,
        out_specs=pl.BlockSpec(memory_space=pl.ANY),
        scratch_shapes=[
            pltpu.VMEM((rows, 2 * CH), jnp.bfloat16),
            pltpu.VMEM((count, feeds, 2 * CH), jnp.bfloat16),
            pltpu.VMEM((TAPS - 1, rows, feeds), jnp.bfloat16),
            pltpu.VMEM((TAPS - 1, rows, feeds), jnp.bfloat16),
            pltpu.VMEM((count, rows, feeds), jnp.float32),
            pltpu.VMEM((owners * GROUPS, tall, feeds), jnp.bfloat16),
            dma,
            dma,
            dma,
        ]
        + [dma((owners,))] * 8,
        compiler_params=pltpu.CompilerParams(
            collective_id=0, has_side_effects=True, vmem_limit_bytes=56 * MIB
        ),
    )(voltage, prototype(), tables(band), flags, owner_slot.reshape(1, band))


def correlate_kernel(inverse, gathered, out):
    feed_groups, owners, _, tall, feeds = gathered.shape
    depth = owners * tall
    first = pl.program_id(1) * out.shape[0]
    own = gathered[lax.axis_index("feed")].reshape(depth, feeds).T
    source = lax.broadcasted_iota(jnp.int32, (depth, depth), 0)
    target = lax.broadcasted_iota(jnp.int32, (depth, depth), 1)
    imag = target // QUAD % 2
    turn = jnp.where(
        source == target + QUAD - 2 * QUAD * imag, (2 * imag - 1).astype(jnp.float32), 0.0
    ).astype(jnp.bfloat16)
    turned = jnp.dot(own, turn, preferred_element_type=jnp.float32).astype(jnp.bfloat16)
    lane = lax.broadcasted_iota(jnp.int32, (1, depth), 1)
    for index in range(out.shape[0]):
        mask = jnp.where(lane % QUAD == first + index, inverse, 0.0).astype(jnp.bfloat16)
        for part, rows in enumerate((own, turned)):
            left = rows * mask
            for group in range(feed_groups):
                out[index, part, :, group * feeds : (group + 1) * feeds] = jnp.dot(
                    left, gathered[group].reshape(depth, feeds), preferred_element_type=jnp.float32
                ).astype(jnp.bfloat16)


def correlate(gathered):
    feed_groups, owners, _, tall, feeds = gathered.shape
    inverse = 1.0 / (owners * tall // (2 * QUAD))
    step = 2
    return pl.pallas_call(
        functools.partial(correlate_kernel, inverse),
        out_shape=jax.ShapeDtypeStruct((CAP, 2, feeds, feed_groups * feeds), jnp.bfloat16),
        grid=(GROUPS, QUAD // step),
        in_specs=[
            pl.BlockSpec((feed_groups, owners, 1, tall, feeds), lambda g, h: (0, 0, g, 0, 0))
        ],
        out_specs=pl.BlockSpec(
            (step, 2, feeds, feed_groups * feeds), lambda g, h: (g * (QUAD // step) + h, 0, 0, 0)
        ),
        compiler_params=pltpu.CompilerParams(vmem_limit_bytes=48 * MIB),
    )(gathered)


def solution(mesh):
    feed_groups, owners = mesh.shape["feed"], mesh.shape["freq"]

    def body(voltage, flags, owner_slot):
        return correlate(spread(voltage, flags, owner_slot, feed_groups, owners))

    placed = (P(None, "feed", "freq"), P("feed", None), P())
    return jax.shard_map(
        body, mesh=mesh, in_specs=placed, out_specs=P("freq", None, "feed", None), check_vma=False
    )
```

```python
import functools
import math

import jax
import jax.numpy as jnp
import ml_dtypes
import numpy as np
from jax import lax
from jax.experimental import pallas as pl
from jax.experimental.pallas import tpu as pltpu
from jax.sharding import PartitionSpec as P

CH = 1024
TAPS = 4
BAND_LO = 256
CAP = 20
QUAD = 4
GROUPS = CAP // QUAD
MESH = pl.DeviceIdType.MESH
MIB = 1024 * 1024


def prototype():
    total = TAPS * CH
    position = np.arange(total, dtype=np.float64)
    taper = 0.5 - 0.5 * np.cos(2 * np.pi * (position + 0.5) / total)
    coeffs = np.sinc((position - total / 2 + 0.5) / CH) * taper
    coeffs = coeffs * np.sqrt(CH / np.sum(coeffs * coeffs))
    return coeffs.reshape(TAPS, CH).astype(np.float32)


def tables(band):
    phase = (np.arange(band)[:, None] + BAND_LO) * np.arange(CH)[None, :] % CH * (2 * np.pi / CH)
    cosine = np.cos(phase).astype(np.float32).astype(ml_dtypes.bfloat16)
    sine = np.sin(phase).astype(np.float32).astype(ml_dtypes.bfloat16)
    return np.concatenate(
        [np.concatenate([cosine, sine], 1), np.concatenate([-sine, cosine], 1)], 0
    )


def spread_kernel(
    count, owners, voltage, coeffs, table, flags, owner_slot, gathered,
    slot_table, weighted, halo_out, halo_in, parts, outgoing,
    halo_send, halo_recv, local_sem, a_send, a_recv, x_send, x_recv, y_send, y_recv, d_send, d_recv,
):
    feed, me = lax.axis_index("feed"), lax.axis_index("freq")
    feeds = voltage.shape[1]
    band = flags.shape[1]
    rows = slot_table.shape[0]
    along_x, along_y = feed ^ 1, feed ^ 2

    barrier = pltpu.get_barrier_semaphore()
    for step in range(1, owners):
        pl.semaphore_signal(barrier, inc=1, device_id=(feed, me ^ step), device_id_type=MESH)
    for other in (along_x, along_y):
        pl.semaphore_signal(barrier, inc=1, device_id=(other, me), device_id_type=MESH)

    row = lax.broadcasted_iota(jnp.int32, (rows, band), 0)
    slot = row // (2 * QUAD) * QUAD + row % QUAD
    kept = jnp.where(slot == owner_slot[...], flags[...].astype(jnp.float32), 0.0)
    kept = kept * (1.0 / math.sqrt(CH))
    imag_row = row // QUAD % 2 == 1
    slot_table[...] = (
        jnp.dot(
            jnp.where(imag_row, 0.0, kept).astype(jnp.bfloat16),
            table[0:band, :],
            preferred_element_type=jnp.float32,
        )
        + jnp.dot(
            jnp.where(imag_row, kept, 0.0).astype(jnp.bfloat16),
            table[band : 2 * band, :],
            preferred_element_type=jnp.float32,
        )
    ).astype(jnp.bfloat16)

    def weigh(sums):
        tall = 32

        @pl.loop(0, feeds // tall)
        def _(index):
            here = pl.ds(pl.multiple_of(index * tall, tall), tall)
            for part in range(2):
                for lane in range(0, CH, 128):
                    blocks = [
                        voltage[part, here, block * CH + lane : block * CH + lane + 128].astype(jnp.float32)
                        for block in range(count)
                    ]
                    for place, pairs in enumerate(sums):
                        total = None
                        for tap, block in pairs:
                            term = blocks[block] * coeffs[tap : tap + 1, lane : lane + 128]
                            total = term if total is None else total + term
                        weighted[place, here, part * CH + lane : part * CH + lane + 128] = total.astype(
                            jnp.bfloat16
                        )

    def transform(place):
        return lax.dot_general(
            slot_table[...],
            weighted[place],
            (((1,), (1,)), ((), ())),
            preferred_element_type=jnp.float32,
        )

    halo = TAPS - 1
    weigh(
        [
            [(tap, spectrum + tap - count) for tap in range(TAPS) if 0 <= spectrum + tap - count < count]
            for spectrum in range(count - halo, count)
        ]
    )

    @pl.loop(0, halo)
    def _(place):
        halo_out[place] = transform(place).astype(jnp.bfloat16)

    pl.semaphore_wait(barrier, owners + 1)
    backward = pltpu.make_async_remote_copy(
        src_ref=halo_out,
        dst_ref=halo_in,
        send_sem=halo_send,
        recv_sem=halo_recv,
        device_id=(feed, jnp.maximum(me - 1, 0)),
        device_id_type=MESH,
    )

    @pl.when(me > 0)
    def _():
        backward.start()

    weigh(
        [
            [(tap, spectrum + tap) for tap in range(TAPS) if spectrum + tap < count]
            for spectrum in range(count)
        ]
    )

    @pl.loop(0, count)
    def _(place):
        parts[place] = transform(place)

    @pl.when(me < owners - 1)
    def _():
        backward.wait_recv()
        for place in range(halo):
            parts[count - halo + place] += halo_in[place].astype(jnp.float32)

    for place in range(0, count, 2):
        pair = [parts[place + k].reshape(rows // 8, 8, feeds) for k in range(2)]
        outgoing[:, place * 8 : place * 8 + 16, :] = jnp.concatenate(pair, 1).astype(jnp.bfloat16)

    def chunk(owner):
        return outgoing.at[pl.ds(owner * GROUPS, GROUPS)]

    keep = pltpu.make_async_copy(chunk(me), gathered.at[feed, me], local_sem)
    keep.start()

    def remote(source, target, send, recv, device):
        return pltpu.make_async_remote_copy(
            src_ref=source, dst_ref=target, send_sem=send, recv_sem=recv, device_id=device, device_id_type=MESH
        )

    to_owner = [None] + [
        remote(chunk(me ^ t), gathered.at[feed, me], a_send.at[t], a_recv.at[t], (feed, me ^ t))
        for t in range(1, owners)
    ]

    def shared(t):
        return chunk(me) if t == 0 else gathered.at[feed, me ^ t]

    to_x = [
        remote(shared(t), gathered.at[feed, me ^ t], x_send.at[t], x_recv.at[t], (along_x, me))
        for t in range(owners)
    ]
    to_y = [
        remote(shared(t), gathered.at[feed, me ^ t], y_send.at[t], y_recv.at[t], (along_y, me))
        for t in range(owners)
    ]
    onward = []
    for t in range(owners):
        origin, target = (along_x, along_y) if t % 2 else (along_y, along_x)
        block = gathered.at[origin, me ^ t]
        onward.append(remote(block, block, d_send.at[t], d_recv.at[t], (target, me)))

    def pass_on(t):
        (to_x if t % 2 else to_y)[t].wait_recv()
        onward[t].start()

    to_x[0].start()
    to_y[0].start()
    for t in range(1, owners):
        to_owner[t].start()
    for t in range(1, owners):
        to_owner[t].wait_recv()
        to_x[t].start()
        to_y[t].start()
        pass_on(t - 1)
    pass_on(owners - 1)

    keep.wait()
    for t in range(owners):
        (to_y if t % 2 else to_x)[t].wait_recv()
        onward[t].wait_recv()
        if t:
            to_owner[t].wait_send()
        to_x[t].wait_send()
        to_y[t].wait_send()
        onward[t].wait_send()

    @pl.when(me > 0)
    def _():
        backward.wait_send()


def spread(voltage, flags, owner_slot, feed_groups, owners):
    feeds, samples = voltage.shape[1:]
    band = flags.shape[1]
    count = samples // CH
    rows = owners * CAP * 2
    tall = count * 2 * QUAD
    vmem = pl.BlockSpec(memory_space=pltpu.VMEM)
    dma = pltpu.SemaphoreType.DMA
    return pl.pallas_call(
        functools.partial(spread_kernel, count, owners),
        out_shape=jax.ShapeDtypeStruct((feed_groups, owners, GROUPS, tall, feeds), jnp.bfloat16),
        in_specs=[vmem] * 5,
        out_specs=pl.BlockSpec(memory_space=pl.ANY),
        scratch_shapes=[
            pltpu.VMEM((rows, 2 * CH), jnp.bfloat16),
            pltpu.VMEM((count, feeds, 2 * CH), jnp.bfloat16),
            pltpu.VMEM((TAPS - 1, rows, feeds), jnp.bfloat16),
            pltpu.VMEM((TAPS - 1, rows, feeds), jnp.bfloat16),
            pltpu.VMEM((count, rows, feeds), jnp.float32),
            pltpu.VMEM((owners * GROUPS, tall, feeds), jnp.bfloat16),
            dma,
            dma,
            dma,
        ]
        + [dma((owners,))] * 8,
        compiler_params=pltpu.CompilerParams(
            collective_id=0, has_side_effects=True, vmem_limit_bytes=56 * MIB
        ),
    )(voltage, prototype(), tables(band), flags, owner_slot.reshape(1, band))


def correlate_kernel(inverse, gathered, out, turn, bases, lefts):
    feed_groups, owners, _, tall, feeds = gathered.shape
    depth = owners * tall
    step = out.shape[0]
    group_id, part_id = pl.program_id(0), pl.program_id(1)

    @pl.when((group_id == 0) & (part_id == 0))
    def _():
        source = lax.broadcasted_iota(jnp.int32, (depth, depth), 0)
        target = lax.broadcasted_iota(jnp.int32, (depth, depth), 1)
        imag = target // QUAD % 2
        turn[...] = jnp.where(
            source == target + QUAD - 2 * QUAD * imag, (2 * imag - 1).astype(jnp.float32), 0.0
        ).astype(jnp.bfloat16)

    @pl.when(part_id == 0)
    def _():
        own = gathered[lax.axis_index("feed")].reshape(depth, feeds).T
        bases[0] = own
        bases[1] = jnp.dot(own, turn[...], preferred_element_type=jnp.float32).astype(jnp.bfloat16)

    lane = lax.broadcasted_iota(jnp.int32, (1, depth), 1)
    for index in range(step):
        mask = jnp.where(lane % QUAD == part_id * step + index, inverse, 0.0).astype(jnp.bfloat16)
        for part in range(2):
            lefts[index, part] = bases[part] * mask
    left = lefts[...].reshape(step * 2 * feeds, depth)
    for group in range(feed_groups):
        product = jnp.dot(left, gathered[group].reshape(depth, feeds), preferred_element_type=jnp.float32)
        out[:, :, :, group * feeds : (group + 1) * feeds] = product.astype(jnp.bfloat16).reshape(
            step, 2, feeds, feeds
        )


def correlate(gathered):
    feed_groups, owners, _, tall, feeds = gathered.shape
    depth = owners * tall
    inverse = 1.0 / (depth // (2 * QUAD))
    step = 2
    return pl.pallas_call(
        functools.partial(correlate_kernel, inverse),
        out_shape=jax.ShapeDtypeStruct((CAP, 2, feeds, feed_groups * feeds), jnp.bfloat16),
        grid=(GROUPS, QUAD // step),
        in_specs=[
            pl.BlockSpec((feed_groups, owners, 1, tall, feeds), lambda g, h: (0, 0, g, 0, 0))
        ],
        out_specs=pl.BlockSpec(
            (step, 2, feeds, feed_groups * feeds), lambda g, h: (g * (QUAD // step) + h, 0, 0, 0)
        ),
        scratch_shapes=[
            pltpu.VMEM((depth, depth), jnp.bfloat16),
            pltpu.VMEM((2, feeds, depth), jnp.bfloat16),
            pltpu.VMEM((step, 2, feeds, depth), jnp.bfloat16),
        ],
        compiler_params=pltpu.CompilerParams(vmem_limit_bytes=62 * MIB),
    )(gathered)


def solution(mesh):
    feed_groups, owners = mesh.shape["feed"], mesh.shape["freq"]

    def body(voltage, flags, owner_slot):
        return correlate(spread(voltage, flags, owner_slot, feed_groups, owners))

    placed = (P(None, "feed", "freq"), P("feed", None), P())
    return jax.shard_map(
        body, mesh=mesh, in_specs=placed, out_specs=P("freq", None, "feed", None), check_vma=False
    )
```

```python
import functools
import math

import jax
import jax.numpy as jnp
import ml_dtypes
import numpy as np
from jax import lax
from jax.experimental import pallas as pl
from jax.experimental.pallas import tpu as pltpu
from jax.sharding import PartitionSpec as P

CH = 1024
TAPS = 4
BAND_LO = 256
CAP = 20
QUAD = 4
GROUPS = CAP // QUAD
HALVES = 2
MESH = pl.DeviceIdType.MESH
MIB = 1024 * 1024


def prototype():
    total = TAPS * CH
    position = np.arange(total, dtype=np.float64)
    taper = 0.5 - 0.5 * np.cos(2 * np.pi * (position + 0.5) / total)
    coeffs = np.sinc((position - total / 2 + 0.5) / CH) * taper
    coeffs = coeffs * np.sqrt(CH / np.sum(coeffs * coeffs))
    return coeffs.reshape(TAPS, CH).astype(np.float32)


def tables(band):
    phase = (np.arange(band)[:, None] + BAND_LO) * np.arange(CH)[None, :] % CH * (2 * np.pi / CH)
    cosine = np.cos(phase).astype(np.float32).astype(ml_dtypes.bfloat16)
    sine = np.sin(phase).astype(np.float32).astype(ml_dtypes.bfloat16)
    return np.concatenate([cosine, sine], 0)


def spread_kernel(
    count, owners, voltage, coeffs, table, flags, owner_slot, gathered,
    samples, slot_table, weighted, halo_out, halo_in, parts, outgoing,
    load_sem, halo_send, halo_recv, local_sem,
    a_send, a_recv, x_send, x_recv, y_send, y_recv, d_send, d_recv,
):
    feed, me = lax.axis_index("feed"), lax.axis_index("freq")
    feeds = samples.shape[2]
    band = flags.shape[1]
    rows = slot_table.shape[0]
    along_x, along_y = feed ^ 1, feed ^ 2
    halo = TAPS - 1

    barrier = pltpu.get_barrier_semaphore()
    for step in range(1, owners):
        pl.semaphore_signal(barrier, inc=1, device_id=(feed, me ^ step), device_id_type=MESH)
    for other in (along_x, along_y):
        pl.semaphore_signal(barrier, inc=1, device_id=(other, me), device_id_type=MESH)

    loads = [
        pltpu.make_async_copy(
            voltage.at[:, half * feeds : (half + 1) * feeds, :], samples.at[half], load_sem.at[half]
        )
        for half in range(HALVES)
    ]
    for load in loads:
        load.start()

    row = lax.broadcasted_iota(jnp.int32, (rows, band), 0)
    slot = row // (2 * QUAD) * QUAD + row % QUAD
    kept = jnp.where(slot == owner_slot[...], flags[...].astype(jnp.float32), 0.0)
    kept = kept * (1.0 / math.sqrt(CH))
    imag_row = row // QUAD % 2 == 1
    real_kept = jnp.where(imag_row, 0.0, kept)
    imag_kept = jnp.where(imag_row, kept, 0.0)
    for part, pick in enumerate(([real_kept, -imag_kept], [imag_kept, real_kept])):
        slot_table[:, part * CH : (part + 1) * CH] = jnp.dot(
            jnp.concatenate(pick, 1).astype(jnp.bfloat16), table[...], preferred_element_type=jnp.float32
        ).astype(jnp.bfloat16)

    def weigh(half, sums):
        tall = 32

        @pl.loop(0, feeds // tall)
        def _(index):
            first = pl.multiple_of(index * tall, tall)
            for part in range(2):
                for lane in range(0, CH, 128):
                    blocks = [
                        samples[
                            half, part, pl.ds(first, tall), block * CH + lane : block * CH + lane + 128
                        ].astype(jnp.float32)
                        for block in range(count)
                    ]
                    for place, pairs in enumerate(sums):
                        total = None
                        for tap, block in pairs:
                            term = blocks[block] * coeffs[tap : tap + 1, lane : lane + 128]
                            total = term if total is None else total + term
                        weighted[
                            pl.ds(place * feeds + first, tall), part * CH + lane : part * CH + lane + 128
                        ] = total.astype(jnp.bfloat16)

    def transform(places):
        return lax.dot_general(
            slot_table[...],
            weighted[0 : places * feeds, :],
            (((1,), (1,)), ((), ())),
            preferred_element_type=jnp.float32,
        )

    def backward(half):
        return pltpu.make_async_remote_copy(
            src_ref=halo_out.at[half],
            dst_ref=halo_in.at[half],
            send_sem=halo_send.at[half],
            recv_sem=halo_recv.at[half],
            device_id=(feed, jnp.maximum(me - 1, 0)),
            device_id_type=MESH,
        )

    def send_halo(half):
        weigh(
            half,
            [
                [(tap, spectrum + tap - count) for tap in range(TAPS) if 0 <= spectrum + tap - count < count]
                for spectrum in range(count - halo, count)
            ],
        )
        halo_out[half] = transform(halo).astype(jnp.bfloat16)
        if half == 0:
            pl.semaphore_wait(barrier, owners + 1)

        @pl.when(me > 0)
        def _():
            backward(half).start()

    def channelize(half):
        weigh(
            half,
            [
                [(tap, spectrum + tap) for tap in range(TAPS) if spectrum + tap < count]
                for spectrum in range(count)
            ],
        )
        parts[...] = transform(count)

    def finish(half):
        @pl.when(me < owners - 1)
        def _():
            backward(half).wait_recv()
            parts[:, (count - halo) * feeds :] += halo_in[half].astype(jnp.float32)

        for place in range(0, count, 2):
            pair = [
                parts[:, (place + k) * feeds : (place + k + 1) * feeds].reshape(rows // 8, 8, feeds)
                for k in range(2)
            ]
            outgoing[half, :, place * 8 : place * 8 + 16, :] = jnp.concatenate(pair, 1).astype(jnp.bfloat16)

    def chunk(half, owner):
        return outgoing.at[half, pl.ds(owner * GROUPS, GROUPS)]

    def remote(source, target, send, recv, device):
        return pltpu.make_async_remote_copy(
            src_ref=source, dst_ref=target, send_sem=send, recv_sem=recv, device_id=device, device_id_type=MESH
        )

    def keep(half):
        return pltpu.make_async_copy(chunk(half, me), gathered.at[feed, half, me], local_sem.at[half])

    def to_owner(half, t):
        return remote(
            chunk(half, me ^ t), gathered.at[feed, half, me],
            a_send.at[half, t], a_recv.at[half, t], (feed, me ^ t),
        )

    def shared(half, t):
        return chunk(half, me) if t == 0 else gathered.at[feed, half, me ^ t]

    def to_x(half, t):
        return remote(
            shared(half, t), gathered.at[feed, half, me ^ t],
            x_send.at[half, t], x_recv.at[half, t], (along_x, me),
        )

    def to_y(half, t):
        return remote(
            shared(half, t), gathered.at[feed, half, me ^ t],
            y_send.at[half, t], y_recv.at[half, t], (along_y, me),
        )

    def onward(half, t):
        origin, target = (along_x, along_y) if t % 2 else (along_y, along_x)
        block = gathered.at[origin, half, me ^ t]
        return remote(block, block, d_send.at[half, t], d_recv.at[half, t], (target, me))

    def pass_on(half, t):
        (to_x if t % 2 else to_y)(half, t).wait_recv()
        onward(half, t).start()

    def send(half):
        to_x(half, 0).start()
        to_y(half, 0).start()
        for t in range(1, owners):
            to_owner(half, t).start()
        keep(half).start()

    loads[0].wait()
    send_halo(0)
    channelize(0)
    loads[1].wait()
    send_halo(1)
    finish(0)
    send(0)
    channelize(1)
    finish(1)
    send(1)

    steps = [(half, t) for half in range(HALVES) for t in range(owners)]
    for before, (half, t) in zip([None] + steps, steps):
        if t:
            to_owner(half, t).wait_recv()
            to_x(half, t).start()
            to_y(half, t).start()
        if before:
            pass_on(*before)
    pass_on(*steps[-1])

    for half, t in steps:
        (to_y if t % 2 else to_x)(half, t).wait_recv()
        onward(half, t).wait_recv()
        if t:
            to_owner(half, t).wait_send()
        to_x(half, t).wait_send()
        to_y(half, t).wait_send()
        onward(half, t).wait_send()
    for half in range(HALVES):
        keep(half).wait()

        @pl.when(me > 0)
        def _():
            backward(half).wait_send()


def spread(voltage, flags, owner_slot, feed_groups, owners):
    feeds, samples = voltage.shape[1:]
    feeds = feeds // HALVES
    band = flags.shape[1]
    count = samples // CH
    rows = owners * CAP * 2
    tall = count * 2 * QUAD
    vmem, anywhere = pl.BlockSpec(memory_space=pltpu.VMEM), pl.BlockSpec(memory_space=pl.ANY)
    dma = pltpu.SemaphoreType.DMA
    return pl.pallas_call(
        functools.partial(spread_kernel, count, owners),
        out_shape=jax.ShapeDtypeStruct(
            (feed_groups, HALVES, owners, GROUPS, tall, feeds), jnp.bfloat16
        ),
        in_specs=[anywhere] + [vmem] * 4,
        out_specs=anywhere,
        scratch_shapes=[
            pltpu.VMEM((HALVES, 2, feeds, samples), jnp.bfloat16),
            pltpu.VMEM((rows, 2 * CH), jnp.bfloat16),
            pltpu.VMEM((count * feeds, 2 * CH), jnp.bfloat16),
            pltpu.VMEM((HALVES, rows, (TAPS - 1) * feeds), jnp.bfloat16),
            pltpu.VMEM((HALVES, rows, (TAPS - 1) * feeds), jnp.bfloat16),
            pltpu.VMEM((rows, count * feeds), jnp.float32),
            pltpu.VMEM((HALVES, owners * GROUPS, tall, feeds), jnp.bfloat16),
        ]
        + [dma((HALVES,))] * 4
        + [dma((HALVES, owners))] * 8,
        compiler_params=pltpu.CompilerParams(
            collective_id=0, has_side_effects=True, vmem_limit_bytes=62 * MIB
        ),
    )(voltage, prototype(), tables(band), flags, owner_slot.reshape(1, band))


def correlate_kernel(inverse, gathered, out, turn, bases):
    feed_groups, halves, owners, _, tall, some = gathered.shape
    depth, feeds = owners * tall, halves * some
    step = out.shape[0]
    group_id, part_id = pl.program_id(0), pl.program_id(1)

    @pl.when((group_id == 0) & (part_id == 0))
    def _():
        source = lax.broadcasted_iota(jnp.int32, (depth, depth), 0)
        target = lax.broadcasted_iota(jnp.int32, (depth, depth), 1)
        imag = target // QUAD % 2
        turn[...] = jnp.where(
            source == target + QUAD - 2 * QUAD * imag, (2 * imag - 1).astype(jnp.float32), 0.0
        ).astype(jnp.bfloat16)

    @pl.when(part_id == 0)
    def _():
        mine = lax.axis_index("feed")
        own = jnp.concatenate([gathered[mine, half].reshape(depth, some).T for half in range(halves)], 0)
        bases[0] = own
        bases[1] = jnp.dot(own, turn[...], preferred_element_type=jnp.float32).astype(jnp.bfloat16)

    lane = lax.broadcasted_iota(jnp.int32, (1, depth), 1)
    right = jnp.concatenate(
        [gathered[group, half].reshape(depth, some) for group in range(feed_groups) for half in range(halves)], 1
    )
    for index in range(step):
        mask = jnp.where(lane % QUAD == part_id * step + index, inverse, 0.0).astype(jnp.bfloat16)
        for part in range(2):
            out[index, part] = jnp.dot(
                bases[part] * mask, right, preferred_element_type=jnp.float32
            ).astype(jnp.bfloat16)


def correlate(gathered):
    feed_groups, halves, owners, _, tall, some = gathered.shape
    depth, feeds = owners * tall, halves * some
    inverse = 1.0 / (depth // (2 * QUAD))
    step = 2
    return pl.pallas_call(
        functools.partial(correlate_kernel, inverse),
        out_shape=jax.ShapeDtypeStruct((CAP, 2, feeds, feed_groups * feeds), jnp.bfloat16),
        grid=(GROUPS, QUAD // step),
        in_specs=[
            pl.BlockSpec((feed_groups, halves, owners, 1, tall, some), lambda g, h: (0, 0, 0, g, 0, 0))
        ],
        out_specs=pl.BlockSpec(
            (step, 2, feeds, feed_groups * feeds), lambda g, h: (g * (QUAD // step) + h, 0, 0, 0)
        ),
        scratch_shapes=[
            pltpu.VMEM((depth, depth), jnp.bfloat16),
            pltpu.VMEM((2, feeds, depth), jnp.bfloat16),
        ],
        compiler_params=pltpu.CompilerParams(vmem_limit_bytes=62 * MIB),
    )(gathered)


def solution(mesh):
    feed_groups, owners = mesh.shape["feed"], mesh.shape["freq"]

    def body(voltage, flags, owner_slot):
        return correlate(spread(voltage, flags, owner_slot, feed_groups, owners))

    placed = (P(None, "feed", "freq"), P("feed", None), P())
    return jax.shard_map(
        body, mesh=mesh, in_specs=placed, out_specs=P("freq", None, "feed", None), check_vma=False
    )
```

```python
import functools
import math

import jax
import jax.numpy as jnp
import ml_dtypes
import numpy as np
from jax import lax
from jax.experimental import pallas as pl
from jax.experimental.pallas import tpu as pltpu
from jax.sharding import PartitionSpec as P

CH = 1024
TAPS = 4
BAND_LO = 256
CAP = 20
QUAD = 4
GROUPS = CAP // QUAD
HALVES = 2
LAG = 3
WINDOW = 4
DEPTH = 2
MESH = pl.DeviceIdType.MESH
MIB = 1024 * 1024


def prototype():
    total = TAPS * CH
    position = np.arange(total, dtype=np.float64)
    taper = 0.5 - 0.5 * np.cos(2 * np.pi * (position + 0.5) / total)
    coeffs = np.sinc((position - total / 2 + 0.5) / CH) * taper
    coeffs = coeffs * np.sqrt(CH / np.sum(coeffs * coeffs))
    return coeffs.reshape(TAPS, CH).astype(np.float32)


def tables(band):
    phase = (np.arange(band)[:, None] + BAND_LO) * np.arange(CH)[None, :] % CH * (2 * np.pi / CH)
    cosine = np.cos(phase).astype(np.float32).astype(ml_dtypes.bfloat16)
    sine = np.sin(phase).astype(np.float32).astype(ml_dtypes.bfloat16)
    return np.concatenate([cosine, sine], 0)


def spread_kernel(
    count, owners, voltage, coeffs, table, flags, owner_slot, gathered,
    samples, slot_table, weighted, halo_out, halo_in, parts, outgoing,
    load_sem, halo_send, halo_recv, local_sem,
    a_send, a_recv, x_send, x_recv, y_send, y_recv, d_send, d_recv,
):
    feed, me = lax.axis_index("feed"), lax.axis_index("freq")
    feeds = samples.shape[2]
    band = flags.shape[1]
    rows = slot_table.shape[0]
    along_x, along_y = feed ^ 1, feed ^ 2
    halo = TAPS - 1

    barrier = pltpu.get_barrier_semaphore()
    for step in range(1, owners):
        pl.semaphore_signal(barrier, inc=1, device_id=(feed, me ^ step), device_id_type=MESH)
    for other in (along_x, along_y):
        pl.semaphore_signal(barrier, inc=1, device_id=(other, me), device_id_type=MESH)

    loads = [
        pltpu.make_async_copy(
            voltage.at[:, half * feeds : (half + 1) * feeds, :], samples.at[half], load_sem.at[half]
        )
        for half in range(HALVES)
    ]
    for load in loads:
        load.start()

    row = lax.broadcasted_iota(jnp.int32, (rows, band), 0)
    slot = row // (2 * QUAD) * QUAD + row % QUAD
    kept = jnp.where(slot == owner_slot[...], flags[...].astype(jnp.float32), 0.0)
    kept = kept * (1.0 / math.sqrt(CH))
    imag_row = row // QUAD % 2 == 1
    real_kept = jnp.where(imag_row, 0.0, kept)
    imag_kept = jnp.where(imag_row, kept, 0.0)
    for part, pick in enumerate(([real_kept, -imag_kept], [imag_kept, real_kept])):
        slot_table[:, part * CH : (part + 1) * CH] = jnp.dot(
            jnp.concatenate(pick, 1).astype(jnp.bfloat16), table[...], preferred_element_type=jnp.float32
        ).astype(jnp.bfloat16)

    def weigh(half, sums):
        tall = 32

        @pl.loop(0, feeds // tall)
        def _(index):
            first = pl.multiple_of(index * tall, tall)
            for part in range(2):
                for lane in range(0, CH, 128):
                    blocks = [
                        samples[
                            half, part, pl.ds(first, tall), block * CH + lane : block * CH + lane + 128
                        ].astype(jnp.float32)
                        for block in range(count)
                    ]
                    for place, pairs in enumerate(sums):
                        total = None
                        for tap, block in pairs:
                            term = blocks[block] * coeffs[tap : tap + 1, lane : lane + 128]
                            total = term if total is None else total + term
                        weighted[
                            pl.ds(place * feeds + first, tall), part * CH + lane : part * CH + lane + 128
                        ] = total.astype(jnp.bfloat16)

    def transform(places):
        return lax.dot_general(
            slot_table[...],
            weighted[0 : places * feeds, :],
            (((1,), (1,)), ((), ())),
            preferred_element_type=jnp.float32,
        )

    def backward(half):
        return pltpu.make_async_remote_copy(
            src_ref=halo_out.at[half],
            dst_ref=halo_in.at[half],
            send_sem=halo_send.at[half],
            recv_sem=halo_recv.at[half],
            device_id=(feed, jnp.maximum(me - 1, 0)),
            device_id_type=MESH,
        )

    def send_halo(half):
        weigh(
            half,
            [
                [(tap, spectrum + tap - count) for tap in range(TAPS) if 0 <= spectrum + tap - count < count]
                for spectrum in range(count - halo, count)
            ],
        )
        halo_out[half] = transform(halo).astype(jnp.bfloat16)
        if half == 0:
            pl.semaphore_wait(barrier, owners + 1)

        @pl.when(me > 0)
        def _():
            backward(half).start()

    def weigh_own(half):
        weigh(
            half,
            [
                [(tap, spectrum + tap) for tap in range(TAPS) if spectrum + tap < count]
                for spectrum in range(count)
            ],
        )

    def transform_own():
        parts[...] = transform(count)

    def finish(half):
        @pl.when(me < owners - 1)
        def _():
            backward(half).wait_recv()
            parts[:, (count - halo) * feeds :] += halo_in[half].astype(jnp.float32)

        for place in range(0, count, 2):
            pair = [
                parts[:, (place + k) * feeds : (place + k + 1) * feeds].reshape(rows // 8, 8, feeds)
                for k in range(2)
            ]
            outgoing[half, :, place * 8 : place * 8 + 16, :] = jnp.concatenate(pair, 1).astype(jnp.bfloat16)

    def chunk(half, owner):
        return outgoing.at[half, pl.ds(owner * GROUPS, GROUPS)]

    def remote(source, target, send, recv, device):
        return pltpu.make_async_remote_copy(
            src_ref=source, dst_ref=target, send_sem=send, recv_sem=recv, device_id=device, device_id_type=MESH
        )

    def keep(half):
        return pltpu.make_async_copy(chunk(half, me), gathered.at[feed, half, me], local_sem.at[half])

    def to_owner(half, t):
        return remote(
            chunk(half, me ^ t), gathered.at[feed, half, me],
            a_send.at[half, t], a_recv.at[half, t], (feed, me ^ t),
        )

    def shared(half, t):
        return chunk(half, me) if t == 0 else gathered.at[feed, half, me ^ t]

    def to_x(half, t):
        return remote(
            shared(half, t), gathered.at[feed, half, me ^ t],
            x_send.at[half, t], x_recv.at[half, t], (along_x, me),
        )

    def to_y(half, t):
        return remote(
            shared(half, t), gathered.at[feed, half, me ^ t],
            y_send.at[half, t], y_recv.at[half, t], (along_y, me),
        )

    def onward(half, t):
        origin, target = (along_x, along_y) if t % 2 else (along_y, along_x)
        block = gathered.at[origin, half, me ^ t]
        return remote(block, block, d_send.at[half, t], d_recv.at[half, t], (target, me))

    def pass_on(half, t):
        (to_x if t % 2 else to_y)(half, t).wait_recv()
        onward(half, t).start()

    steps = sorted(
        [(half, t) for half in range(HALVES) for t in range(owners)],
        key=lambda step: (step[1] + LAG * step[0], -step[0]),
    )
    early = [(0, t) for t in range(min(LAG + 1, owners))] if HALVES > 1 else []
    steps = early + [step for step in steps if step not in early]
    leaving = [step for step in steps if step[1]]
    handled = []

    def leave(half, limit):
        ready = [step for step in leaving if step[0] <= half][:limit]
        for step in ready:
            leaving.remove(step)
            to_owner(*step).start()

    def handle(step, ready):
        half, t = step
        if t:
            assert step not in leaving
            to_owner(half, t).wait_recv()
            leave(ready, 1)
        to_x(half, t).start()
        to_y(half, t).start()
        handled.append(step)
        if len(handled) > DEPTH:
            pass_on(*handled[-1 - DEPTH])

    loads[0].wait()
    send_halo(0)
    weigh_own(0)
    transform_own()
    for half in range(1, HALVES):
        loads[half].wait()
        send_halo(half)
    finish(0)
    keep(0).start()
    if HALVES == 1:
        handle(steps[0], 0)
        leave(0, WINDOW)
    else:
        handle(early[0], 0)
        leave(0, WINDOW)
        weigh_own(1)
        handle(early[1], 0)
        transform_own()
        for step in early[2:]:
            handle(step, 0)
        finish(1)
        keep(1).start()
        handle((1, 0), 1)
        leave(1, WINDOW)
    for step in steps:
        if step not in handled:
            handle(step, HALVES - 1)
    for step in handled[-DEPTH:]:
        pass_on(*step)

    for half, t in steps:
        (to_y if t % 2 else to_x)(half, t).wait_recv()
        onward(half, t).wait_recv()
        if t:
            to_owner(half, t).wait_send()
        to_x(half, t).wait_send()
        to_y(half, t).wait_send()
        onward(half, t).wait_send()
    for half in range(HALVES):
        keep(half).wait()

        @pl.when(me > 0)
        def _():
            backward(half).wait_send()


def spread(voltage, flags, owner_slot, feed_groups, owners):
    feeds, samples = voltage.shape[1:]
    feeds = feeds // HALVES
    band = flags.shape[1]
    count = samples // CH
    rows = owners * CAP * 2
    tall = count * 2 * QUAD
    vmem, anywhere = pl.BlockSpec(memory_space=pltpu.VMEM), pl.BlockSpec(memory_space=pl.ANY)
    dma = pltpu.SemaphoreType.DMA
    return pl.pallas_call(
        functools.partial(spread_kernel, count, owners),
        out_shape=jax.ShapeDtypeStruct(
            (feed_groups, HALVES, owners, GROUPS, tall, feeds), jnp.bfloat16
        ),
        in_specs=[anywhere] + [vmem] * 4,
        out_specs=anywhere,
        scratch_shapes=[
            pltpu.VMEM((HALVES, 2, feeds, samples), jnp.bfloat16),
            pltpu.VMEM((rows, 2 * CH), jnp.bfloat16),
            pltpu.VMEM((count * feeds, 2 * CH), jnp.bfloat16),
            pltpu.VMEM((HALVES, rows, (TAPS - 1) * feeds), jnp.bfloat16),
            pltpu.VMEM((HALVES, rows, (TAPS - 1) * feeds), jnp.bfloat16),
            pltpu.VMEM((rows, count * feeds), jnp.float32),
            pltpu.VMEM((HALVES, owners * GROUPS, tall, feeds), jnp.bfloat16),
        ]
        + [dma((HALVES,))] * 4
        + [dma((HALVES, owners))] * 8,
        compiler_params=pltpu.CompilerParams(
            collective_id=0, has_side_effects=True, vmem_limit_bytes=62 * MIB
        ),
    )(voltage, prototype(), tables(band), flags, owner_slot.reshape(1, band))


def correlate_kernel(inverse, gathered, out, held, turn, bases, results, in_sem, out_sem):
    _, feed_groups, halves, owners, tall, some = held.shape
    depth = owners * tall

    def fetch(group):
        return pltpu.make_async_copy(gathered.at[:, :, :, group], held.at[group], in_sem.at[group])

    def store(slot, part):
        return pltpu.make_async_copy(results.at[slot, part], out.at[slot, part], out_sem.at[slot, part])

    for group in range(GROUPS):
        fetch(group).start()
    source = lax.broadcasted_iota(jnp.int32, (depth, depth), 0)
    target = lax.broadcasted_iota(jnp.int32, (depth, depth), 1)
    imag = target // QUAD % 2
    turn[...] = jnp.where(
        source == target + QUAD - 2 * QUAD * imag, (2 * imag - 1).astype(jnp.float32), 0.0
    ).astype(jnp.bfloat16)
    lane = lax.broadcasted_iota(jnp.int32, (1, depth), 1)
    mine = lax.axis_index("feed")

    @pl.loop(0, GROUPS)
    def _(group):
        fetch(group).wait()
        own = jnp.concatenate([held[group, mine, half].reshape(depth, some).T for half in range(halves)], 0)
        bases[0] = own
        bases[1] = jnp.dot(own, turn[...], preferred_element_type=jnp.float32).astype(jnp.bfloat16)
        right = jnp.concatenate(
            [held[group, other, half].reshape(depth, some) for other in range(feed_groups) for half in range(halves)],
            1,
        )
        for index in range(QUAD):
            slot = group * QUAD + index
            mask = jnp.where(lane % QUAD == index, inverse, 0.0).astype(jnp.bfloat16)
            for part in range(2):
                results[slot, part] = jnp.dot(
                    bases[part] * mask, right, preferred_element_type=jnp.float32
                ).astype(jnp.bfloat16)
                store(slot, part).start()

    @pl.loop(0, CAP)
    def _(slot):
        for part in range(2):
            store(slot, part).wait()


def correlate(gathered):
    feed_groups, halves, owners, _, tall, some = gathered.shape
    depth, feeds = owners * tall, halves * some
    inverse = 1.0 / (depth // (2 * QUAD))
    shape = (CAP, 2, feeds, feed_groups * feeds)
    anywhere = pl.BlockSpec(memory_space=pl.ANY)
    return pl.pallas_call(
        functools.partial(correlate_kernel, inverse),
        out_shape=jax.ShapeDtypeStruct(shape, jnp.bfloat16),
        in_specs=[anywhere],
        out_specs=anywhere,
        scratch_shapes=[
            pltpu.VMEM((GROUPS, feed_groups, halves, owners, tall, some), jnp.bfloat16),
            pltpu.VMEM((depth, depth), jnp.bfloat16),
            pltpu.VMEM((2, feeds, depth), jnp.bfloat16),
            pltpu.VMEM(shape, jnp.bfloat16),
            pltpu.SemaphoreType.DMA((GROUPS,)),
            pltpu.SemaphoreType.DMA((CAP, 2)),
        ],
        compiler_params=pltpu.CompilerParams(vmem_limit_bytes=62 * MIB),
    )(gathered)


def solution(mesh):
    feed_groups, owners = mesh.shape["feed"], mesh.shape["freq"]

    def body(voltage, flags, owner_slot):
        return correlate(spread(voltage, flags, owner_slot, feed_groups, owners))

    placed = (P(None, "feed", "freq"), P("feed", None), P())
    return jax.shard_map(
        body, mesh=mesh, in_specs=placed, out_specs=P("freq", None, "feed", None), check_vma=False
    )
```

```python
import functools
import math

import jax
import jax.numpy as jnp
import ml_dtypes
import numpy as np
from jax import lax
from jax.experimental import pallas as pl
from jax.experimental.pallas import tpu as pltpu
from jax.sharding import PartitionSpec as P

CH = 1024
TAPS = 4
BAND_LO = 256
CAP = 20
QUAD = 4
GROUPS = CAP // QUAD
HALVES = 1
LOADS = 4
LAG = 3
WINDOW = 4
DEPTH = 2
MESH = pl.DeviceIdType.MESH
MIB = 1024 * 1024


def prototype():
    total = TAPS * CH
    position = np.arange(total, dtype=np.float64)
    taper = 0.5 - 0.5 * np.cos(2 * np.pi * (position + 0.5) / total)
    coeffs = np.sinc((position - total / 2 + 0.5) / CH) * taper
    coeffs = coeffs * np.sqrt(CH / np.sum(coeffs * coeffs))
    return coeffs.reshape(TAPS, CH).astype(np.float32)


def tables(band):
    phase = (np.arange(band)[:, None] + BAND_LO) * np.arange(CH)[None, :] % CH * (2 * np.pi / CH)
    cosine = np.cos(phase).astype(np.float32).astype(ml_dtypes.bfloat16)
    sine = np.sin(phase).astype(np.float32).astype(ml_dtypes.bfloat16)
    return np.concatenate([cosine, sine], 0)


def spread_kernel(
    count, owners, voltage, coeffs, table_hbm, flags, owner_slot, gathered,
    samples, table, slot_table, weighted, halo_out, halo_in, parts, outgoing,
    load_sem, table_sem, halo_send, halo_recv, local_sem,
    a_send, a_recv, x_send, x_recv, y_send, y_recv, d_send, d_recv,
):
    feed, me = lax.axis_index("feed"), lax.axis_index("freq")
    feeds = samples.shape[1] // HALVES
    band = flags.shape[1]
    rows = slot_table.shape[0]
    along_x, along_y = feed ^ 1, feed ^ 2
    halo = TAPS - 1

    barrier = pltpu.get_barrier_semaphore()
    for step in range(1, owners):
        pl.semaphore_signal(barrier, inc=1, device_id=(feed, me ^ step), device_id_type=MESH)
    for other in (along_x, along_y):
        pl.semaphore_signal(barrier, inc=1, device_id=(other, me), device_id_type=MESH)

    tables_in = pltpu.make_async_copy(table_hbm, table, table_sem)
    tables_in.start()
    share = samples.shape[1] // LOADS

    def load(index):
        here = slice(index * share, (index + 1) * share)
        return pltpu.make_async_copy(voltage.at[:, here, :], samples.at[:, here, :], load_sem.at[index])

    for index in range(LOADS):
        load(index).start()

    row = lax.broadcasted_iota(jnp.int32, (rows, band), 0)
    slot = row // (2 * QUAD) * QUAD + row % QUAD
    kept = jnp.where(slot == owner_slot[...], flags[...].astype(jnp.float32), 0.0)
    kept = kept * (1.0 / math.sqrt(CH))
    imag_row = row // QUAD % 2 == 1
    real_kept = jnp.where(imag_row, 0.0, kept)
    imag_kept = jnp.where(imag_row, kept, 0.0)
    tables_in.wait()
    for part, pick in enumerate(([real_kept, -imag_kept], [imag_kept, real_kept])):
        slot_table[:, part * CH : (part + 1) * CH] = jnp.dot(
            jnp.concatenate(pick, 1).astype(jnp.bfloat16), table[...], preferred_element_type=jnp.float32
        ).astype(jnp.bfloat16)

    sums = [
        [(tap, spectrum + tap - count) for tap in range(TAPS) if 0 <= spectrum + tap - count < count]
        for spectrum in range(count - halo, count)
    ] + [[(tap, spectrum + tap) for tap in range(TAPS) if spectrum + tap < count] for spectrum in range(count)]

    def weigh(half):
        tall = 32
        for index in range(half * LOADS // HALVES, (half + 1) * LOADS // HALVES):
            load(index).wait()

            @pl.loop(0, share // tall)
            def _(step):
                first = pl.multiple_of(index * share + step * tall, tall)
                placed = first - half * feeds
                for part in range(2):
                    for lane in range(0, CH, 128):
                        blocks = [
                            samples[
                                part, pl.ds(first, tall), block * CH + lane : block * CH + lane + 128
                            ].astype(jnp.float32)
                            for block in range(count)
                        ]
                        for place, pairs in enumerate(sums):
                            total = None
                            for tap, block in pairs:
                                term = blocks[block] * coeffs[tap : tap + 1, lane : lane + 128]
                                total = term if total is None else total + term
                            weighted[
                                pl.ds(pl.multiple_of(place * feeds + placed, tall), tall),
                                part * CH + lane : part * CH + lane + 128,
                            ] = total.astype(jnp.bfloat16)

    def transform(start, stop):
        return lax.dot_general(
            slot_table[...],
            weighted[start * feeds : stop * feeds, :],
            (((1,), (1,)), ((), ())),
            preferred_element_type=jnp.float32,
        )

    def backward(half):
        return pltpu.make_async_remote_copy(
            src_ref=halo_out.at[half],
            dst_ref=halo_in.at[half],
            send_sem=halo_send.at[half],
            recv_sem=halo_recv.at[half],
            device_id=(feed, jnp.maximum(me - 1, 0)),
            device_id_type=MESH,
        )

    def send_halo(half):
        halo_out[half] = transform(0, halo).astype(jnp.bfloat16)
        if half == 0:
            pl.semaphore_wait(barrier, owners + 1)

        @pl.when(me > 0)
        def _():
            backward(half).start()

    def transform_own():
        parts[...] = transform(halo, halo + count)

    def finish(half):
        @pl.when(me < owners - 1)
        def _():
            backward(half).wait_recv()
            parts[:, (count - halo) * feeds :] += halo_in[half].astype(jnp.float32)

        for place in range(0, count, 2):
            pair = [
                parts[:, (place + k) * feeds : (place + k + 1) * feeds].reshape(rows // 8, 8, feeds)
                for k in range(2)
            ]
            outgoing[half, :, place * 8 : place * 8 + 16, :] = jnp.concatenate(pair, 1).astype(jnp.bfloat16)

    def chunk(half, owner):
        return outgoing.at[half, pl.ds(owner * GROUPS, GROUPS)]

    def remote(source, target, send, recv, device):
        return pltpu.make_async_remote_copy(
            src_ref=source, dst_ref=target, send_sem=send, recv_sem=recv, device_id=device, device_id_type=MESH
        )

    def keep(half):
        return pltpu.make_async_copy(chunk(half, me), gathered.at[feed, half, me], local_sem.at[half])

    def to_owner(half, t):
        return remote(
            chunk(half, me ^ t), gathered.at[feed, half, me],
            a_send.at[half, t], a_recv.at[half, t], (feed, me ^ t),
        )

    def shared(half, t):
        return chunk(half, me) if t == 0 else gathered.at[feed, half, me ^ t]

    def to_x(half, t):
        return remote(
            shared(half, t), gathered.at[feed, half, me ^ t],
            x_send.at[half, t], x_recv.at[half, t], (along_x, me),
        )

    def to_y(half, t):
        return remote(
            shared(half, t), gathered.at[feed, half, me ^ t],
            y_send.at[half, t], y_recv.at[half, t], (along_y, me),
        )

    def onward(half, t):
        origin, target = (along_x, along_y) if t % 2 else (along_y, along_x)
        block = gathered.at[origin, half, me ^ t]
        return remote(block, block, d_send.at[half, t], d_recv.at[half, t], (target, me))

    def pass_on(half, t):
        (to_x if t % 2 else to_y)(half, t).wait_recv()
        onward(half, t).start()

    steps = sorted(
        [(half, t) for half in range(HALVES) for t in range(owners)],
        key=lambda step: (step[1] + LAG * step[0], -step[0]),
    )
    early = [(0, t) for t in range(min(LAG + 1, owners))] if HALVES > 1 else []
    steps = early + [step for step in steps if step not in early]
    leaving = [step for step in steps if step[1]]
    handled = []

    def leave(half, limit):
        ready = [step for step in leaving if step[0] <= half][:limit]
        for step in ready:
            leaving.remove(step)
            to_owner(*step).start()

    def handle(step, ready):
        half, t = step
        if t:
            assert step not in leaving
            to_owner(half, t).wait_recv()
            leave(ready, 1)
        to_x(half, t).start()
        to_y(half, t).start()
        handled.append(step)
        if len(handled) > DEPTH:
            pass_on(*handled[-1 - DEPTH])

    weigh(0)
    send_halo(0)
    transform_own()
    if HALVES > 1:
        weigh(1)
        send_halo(1)
    finish(0)
    keep(0).start()
    handle((0, 0), 0)
    leave(0, WINDOW)
    if HALVES > 1:
        transform_own()
        for step in early[1:]:
            handle(step, 0)
        finish(1)
        keep(1).start()
        handle((1, 0), 1)
        leave(1, WINDOW)
    for step in steps:
        if step not in handled:
            handle(step, HALVES - 1)
    for step in handled[-DEPTH:]:
        pass_on(*step)

    for half, t in steps:
        (to_y if t % 2 else to_x)(half, t).wait_recv()
        onward(half, t).wait_recv()
        if t:
            to_owner(half, t).wait_send()
        to_x(half, t).wait_send()
        to_y(half, t).wait_send()
        onward(half, t).wait_send()
    for half in range(HALVES):
        keep(half).wait()

        @pl.when(me > 0)
        def _():
            backward(half).wait_send()


def spread(voltage, flags, owner_slot, feed_groups, owners):
    feeds, samples = voltage.shape[1:]
    feeds = feeds // HALVES
    band = flags.shape[1]
    count = samples // CH
    rows = owners * CAP * 2
    tall = count * 2 * QUAD
    vmem, anywhere = pl.BlockSpec(memory_space=pltpu.VMEM), pl.BlockSpec(memory_space=pl.ANY)
    dma = pltpu.SemaphoreType.DMA
    return pl.pallas_call(
        functools.partial(spread_kernel, count, owners),
        out_shape=jax.ShapeDtypeStruct(
            (feed_groups, HALVES, owners, GROUPS, tall, feeds), jnp.bfloat16
        ),
        in_specs=[anywhere, vmem, anywhere, vmem, vmem],
        out_specs=anywhere,
        scratch_shapes=[
            pltpu.VMEM((2, HALVES * feeds, samples), jnp.bfloat16),
            pltpu.VMEM((2 * band, CH), jnp.bfloat16),
            pltpu.VMEM((rows, 2 * CH), jnp.bfloat16),
            pltpu.VMEM(((count + TAPS - 1) * feeds, 2 * CH), jnp.bfloat16),
            pltpu.VMEM((HALVES, rows, (TAPS - 1) * feeds), jnp.bfloat16),
            pltpu.VMEM((HALVES, rows, (TAPS - 1) * feeds), jnp.bfloat16),
            pltpu.VMEM((rows, count * feeds), jnp.float32),
            pltpu.VMEM((HALVES, owners * GROUPS, tall, feeds), jnp.bfloat16),
        ]
        + [dma((LOADS,)), dma]
        + [dma((HALVES,))] * 3
        + [dma((HALVES, owners))] * 8,
        compiler_params=pltpu.CompilerParams(
            collective_id=0, has_side_effects=True, vmem_limit_bytes=62 * MIB
        ),
    )(voltage, prototype(), tables(band), flags, owner_slot.reshape(1, band))


def correlate_kernel(inverse, gathered, out, held, turn, bases, results, in_sem, out_sem):
    _, feed_groups, halves, owners, tall, some = held.shape
    depth = owners * tall

    def fetch(group):
        return pltpu.make_async_copy(gathered.at[:, :, :, group], held.at[group], in_sem.at[group])

    def store(slot, part):
        return pltpu.make_async_copy(results.at[slot, part], out.at[slot, part], out_sem.at[slot, part])

    fetch(0).start()
    source = lax.broadcasted_iota(jnp.int32, (depth, depth), 0)
    target = lax.broadcasted_iota(jnp.int32, (depth, depth), 1)
    imag = target // QUAD % 2
    turn[...] = jnp.where(
        source == target + QUAD - 2 * QUAD * imag, (2 * imag - 1).astype(jnp.float32), 0.0
    ).astype(jnp.bfloat16)
    lane = lax.broadcasted_iota(jnp.int32, (1, depth), 1)
    mine = lax.axis_index("feed")
    fetch(0).wait()
    for group in range(1, GROUPS):
        fetch(group).start()

    @pl.loop(0, GROUPS)
    def _(group):
        @pl.when(group > 0)
        def _():
            fetch(group).wait()

        own = jnp.concatenate([held[group, mine, half].reshape(depth, some).T for half in range(halves)], 0)
        bases[0] = own
        bases[1] = jnp.dot(own, turn[...], preferred_element_type=jnp.float32).astype(jnp.bfloat16)
        right = jnp.concatenate(
            [held[group, other, half].reshape(depth, some) for other in range(feed_groups) for half in range(halves)],
            1,
        )
        for index in range(QUAD):
            slot = group * QUAD + index
            mask = jnp.where(lane % QUAD == index, inverse, 0.0).astype(jnp.bfloat16)
            for part in range(2):
                results[slot, part] = jnp.dot(
                    bases[part] * mask, right, preferred_element_type=jnp.float32
                ).astype(jnp.bfloat16)
                store(slot, part).start()

    @pl.loop(0, CAP)
    def _(slot):
        for part in range(2):
            store(slot, part).wait()


def correlate(gathered):
    feed_groups, halves, owners, _, tall, some = gathered.shape
    depth, feeds = owners * tall, halves * some
    inverse = 1.0 / (depth // (2 * QUAD))
    shape = (CAP, 2, feeds, feed_groups * feeds)
    anywhere = pl.BlockSpec(memory_space=pl.ANY)
    return pl.pallas_call(
        functools.partial(correlate_kernel, inverse),
        out_shape=jax.ShapeDtypeStruct(shape, jnp.bfloat16),
        in_specs=[anywhere],
        out_specs=anywhere,
        scratch_shapes=[
            pltpu.VMEM((GROUPS, feed_groups, halves, owners, tall, some), jnp.bfloat16),
            pltpu.VMEM((depth, depth), jnp.bfloat16),
            pltpu.VMEM((2, feeds, depth), jnp.bfloat16),
            pltpu.VMEM(shape, jnp.bfloat16),
            pltpu.SemaphoreType.DMA((GROUPS,)),
            pltpu.SemaphoreType.DMA((CAP, 2)),
        ],
        compiler_params=pltpu.CompilerParams(vmem_limit_bytes=62 * MIB),
    )(gathered)


def solution(mesh):
    feed_groups, owners = mesh.shape["feed"], mesh.shape["freq"]

    def body(voltage, flags, owner_slot):
        return correlate(spread(voltage, flags, owner_slot, feed_groups, owners))

    placed = (P(None, "feed", "freq"), P("feed", None), P())
    return jax.shard_map(
        body, mesh=mesh, in_specs=placed, out_specs=P("freq", None, "feed", None), check_vma=False
    )
```

```python
import functools
import math

import jax
import jax.numpy as jnp
import ml_dtypes
import numpy as np
from jax import lax
from jax.experimental import pallas as pl
from jax.experimental.pallas import tpu as pltpu
from jax.sharding import PartitionSpec as P

CH = 1024
TAPS = 4
BAND_LO = 256
CAP = 20
QUAD = 4
GROUPS = CAP // QUAD
HALVES = 2
LOADS = 4
LAG = 3
WINDOW = 1024
DEPTH = 3
MESH = pl.DeviceIdType.MESH
MIB = 1024 * 1024


def prototype():
    total = TAPS * CH
    position = np.arange(total, dtype=np.float64)
    taper = 0.5 - 0.5 * np.cos(2 * np.pi * (position + 0.5) / total)
    coeffs = np.sinc((position - total / 2 + 0.5) / CH) * taper
    coeffs = coeffs * np.sqrt(CH / np.sum(coeffs * coeffs))
    return coeffs.reshape(TAPS, CH).astype(np.float32)


def tables(band):
    phase = (np.arange(band)[:, None] + BAND_LO) * np.arange(CH)[None, :] % CH * (2 * np.pi / CH)
    cosine = np.cos(phase).astype(np.float32).astype(ml_dtypes.bfloat16)
    sine = np.sin(phase).astype(np.float32).astype(ml_dtypes.bfloat16)
    return np.concatenate([cosine, sine], 0)


def spread_kernel(
    count, owners, voltage, coeffs, table_hbm, flags, owner_slot, gathered,
    samples, table, slot_table, weighted, halo_out, halo_in, parts, outgoing,
    load_sem, table_sem, halo_send, halo_recv, local_sem,
    a_send, a_recv, x_send, x_recv, y_send, y_recv, d_send, d_recv,
):
    feed, me = lax.axis_index("feed"), lax.axis_index("freq")
    feeds = samples.shape[1] // HALVES
    band = flags.shape[1]
    rows = slot_table.shape[0]
    along_x, along_y = feed ^ 1, feed ^ 2
    halo = TAPS - 1

    barrier = pltpu.get_barrier_semaphore()
    for step in range(1, owners):
        pl.semaphore_signal(barrier, inc=1, device_id=(feed, me ^ step), device_id_type=MESH)
    for other in (along_x, along_y):
        pl.semaphore_signal(barrier, inc=1, device_id=(other, me), device_id_type=MESH)

    tables_in = pltpu.make_async_copy(table_hbm, table, table_sem)
    tables_in.start()
    share = samples.shape[1] // LOADS

    def load(index):
        here = slice(index * share, (index + 1) * share)
        return pltpu.make_async_copy(voltage.at[:, here, :], samples.at[:, here, :], load_sem.at[index])

    for index in range(LOADS):
        load(index).start()

    row = lax.broadcasted_iota(jnp.int32, (rows, band), 0)
    slot = row // (2 * QUAD) * QUAD + row % QUAD
    kept = jnp.where(slot == owner_slot[...], flags[...].astype(jnp.float32), 0.0)
    kept = kept * (1.0 / math.sqrt(CH))
    imag_row = row // QUAD % 2 == 1
    real_kept = jnp.where(imag_row, 0.0, kept)
    imag_kept = jnp.where(imag_row, kept, 0.0)
    tables_in.wait()
    for part, pick in enumerate(([real_kept, -imag_kept], [imag_kept, real_kept])):
        slot_table[:, part * CH : (part + 1) * CH] = jnp.dot(
            jnp.concatenate(pick, 1).astype(jnp.bfloat16), table[...], preferred_element_type=jnp.float32
        ).astype(jnp.bfloat16)

    sums = [
        [(tap, spectrum + tap - count) for tap in range(TAPS) if 0 <= spectrum + tap - count < count]
        for spectrum in range(count - halo, count)
    ] + [[(tap, spectrum + tap) for tap in range(TAPS) if spectrum + tap < count] for spectrum in range(count)]

    def weigh(half):
        tall = 32
        for index in range(half * LOADS // HALVES, (half + 1) * LOADS // HALVES):
            load(index).wait()

            @pl.loop(0, share // tall)
            def _(step):
                first = pl.multiple_of(index * share + step * tall, tall)
                placed = first - half * feeds
                for part in range(2):
                    for lane in range(0, CH, 128):
                        blocks = [
                            samples[
                                part, pl.ds(first, tall), block * CH + lane : block * CH + lane + 128
                            ].astype(jnp.float32)
                            for block in range(count)
                        ]
                        for place, pairs in enumerate(sums):
                            total = None
                            for tap, block in pairs:
                                term = blocks[block] * coeffs[tap : tap + 1, lane : lane + 128]
                                total = term if total is None else total + term
                            weighted[
                                pl.ds(pl.multiple_of(place * feeds + placed, tall), tall),
                                part * CH + lane : part * CH + lane + 128,
                            ] = total.astype(jnp.bfloat16)

    def transform(start, stop):
        return lax.dot_general(
            slot_table[...],
            weighted[start * feeds : stop * feeds, :],
            (((1,), (1,)), ((), ())),
            preferred_element_type=jnp.float32,
        )

    def backward(half):
        return pltpu.make_async_remote_copy(
            src_ref=halo_out.at[half],
            dst_ref=halo_in.at[half],
            send_sem=halo_send.at[half],
            recv_sem=halo_recv.at[half],
            device_id=(feed, jnp.maximum(me - 1, 0)),
            device_id_type=MESH,
        )

    def send_halo(half):
        halo_out[half] = transform(0, halo).astype(jnp.bfloat16)
        if half == 0:
            pl.semaphore_wait(barrier, owners + 1)

        @pl.when(me > 0)
        def _():
            backward(half).start()

    def transform_own():
        parts[...] = transform(halo, halo + count)

    def finish(half):
        @pl.when(me < owners - 1)
        def _():
            backward(half).wait_recv()
            parts[:, (count - halo) * feeds :] += halo_in[half].astype(jnp.float32)

        for place in range(0, count, 2):
            pair = [
                parts[:, (place + k) * feeds : (place + k + 1) * feeds].reshape(rows // 8, 8, feeds)
                for k in range(2)
            ]
            outgoing[half, :, place * 8 : place * 8 + 16, :] = jnp.concatenate(pair, 1).astype(jnp.bfloat16)

    def chunk(half, owner):
        return outgoing.at[half, pl.ds(owner * GROUPS, GROUPS)]

    def remote(source, target, send, recv, device):
        return pltpu.make_async_remote_copy(
            src_ref=source, dst_ref=target, send_sem=send, recv_sem=recv, device_id=device, device_id_type=MESH
        )

    def keep(half):
        return pltpu.make_async_copy(chunk(half, me), gathered.at[feed, half, me], local_sem.at[half])

    def to_owner(half, t):
        return remote(
            chunk(half, me ^ t), gathered.at[feed, half, me],
            a_send.at[half, t], a_recv.at[half, t], (feed, me ^ t),
        )

    def shared(half, t):
        return chunk(half, me) if t == 0 else gathered.at[feed, half, me ^ t]

    def to_x(half, t):
        return remote(
            shared(half, t), gathered.at[feed, half, me ^ t],
            x_send.at[half, t], x_recv.at[half, t], (along_x, me),
        )

    def to_y(half, t):
        return remote(
            shared(half, t), gathered.at[feed, half, me ^ t],
            y_send.at[half, t], y_recv.at[half, t], (along_y, me),
        )

    def onward(half, t):
        origin, target = (along_x, along_y) if t % 2 else (along_y, along_x)
        block = gathered.at[origin, half, me ^ t]
        return remote(block, block, d_send.at[half, t], d_recv.at[half, t], (target, me))

    def pass_on(half, t):
        (to_x if t % 2 else to_y)(half, t).wait_recv()
        onward(half, t).start()

    steps = sorted(
        [(half, t) for half in range(HALVES) for t in range(owners)],
        key=lambda step: (step[1] + LAG * step[0], -step[0]),
    )
    early = [(0, t) for t in range(min(LAG + 1, owners))] if HALVES > 1 else []
    steps = early + [step for step in steps if step not in early]
    leaving = [step for step in steps if step[1]]
    handled = []

    def leave(half, limit):
        ready = [step for step in leaving if step[0] <= half][:limit]
        for step in ready:
            leaving.remove(step)
            to_owner(*step).start()

    def handle(step, ready):
        half, t = step
        if t:
            assert step not in leaving
            to_owner(half, t).wait_recv()
            leave(ready, 1)
        to_x(half, t).start()
        to_y(half, t).start()
        handled.append(step)
        if len(handled) > DEPTH:
            pass_on(*handled[-1 - DEPTH])

    weigh(0)
    send_halo(0)
    transform_own()
    if HALVES > 1:
        weigh(1)
        send_halo(1)
    finish(0)
    keep(0).start()
    handle((0, 0), 0)
    leave(0, WINDOW)
    if HALVES > 1:
        transform_own()
        for step in early[1:]:
            handle(step, 0)
        finish(1)
        keep(1).start()
        handle((1, 0), 1)
        leave(1, WINDOW)
    for step in steps:
        if step not in handled:
            handle(step, HALVES - 1)
    for step in handled[-DEPTH:]:
        pass_on(*step)

    for half, t in steps:
        (to_y if t % 2 else to_x)(half, t).wait_recv()
        onward(half, t).wait_recv()
        if t:
            to_owner(half, t).wait_send()
        to_x(half, t).wait_send()
        to_y(half, t).wait_send()
        onward(half, t).wait_send()
    for half in range(HALVES):
        keep(half).wait()

        @pl.when(me > 0)
        def _():
            backward(half).wait_send()


def spread(voltage, flags, owner_slot, feed_groups, owners):
    feeds, samples = voltage.shape[1:]
    feeds = feeds // HALVES
    band = flags.shape[1]
    count = samples // CH
    rows = owners * CAP * 2
    tall = count * 2 * QUAD
    vmem, anywhere = pl.BlockSpec(memory_space=pltpu.VMEM), pl.BlockSpec(memory_space=pl.ANY)
    dma = pltpu.SemaphoreType.DMA
    return pl.pallas_call(
        functools.partial(spread_kernel, count, owners),
        out_shape=jax.ShapeDtypeStruct(
            (feed_groups, HALVES, owners, GROUPS, tall, feeds), jnp.bfloat16
        ),
        in_specs=[anywhere, vmem, anywhere, vmem, vmem],
        out_specs=anywhere,
        scratch_shapes=[
            pltpu.VMEM((2, HALVES * feeds, samples), jnp.bfloat16),
            pltpu.VMEM((2 * band, CH), jnp.bfloat16),
            pltpu.VMEM((rows, 2 * CH), jnp.bfloat16),
            pltpu.VMEM(((count + TAPS - 1) * feeds, 2 * CH), jnp.bfloat16),
            pltpu.VMEM((HALVES, rows, (TAPS - 1) * feeds), jnp.bfloat16),
            pltpu.VMEM((HALVES, rows, (TAPS - 1) * feeds), jnp.bfloat16),
            pltpu.VMEM((rows, count * feeds), jnp.float32),
            pltpu.VMEM((HALVES, owners * GROUPS, tall, feeds), jnp.bfloat16),
        ]
        + [dma((LOADS,)), dma]
        + [dma((HALVES,))] * 3
        + [dma((HALVES, owners))] * 8,
        compiler_params=pltpu.CompilerParams(
            collective_id=0, has_side_effects=True, vmem_limit_bytes=62 * MIB
        ),
    )(voltage, prototype(), tables(band), flags, owner_slot.reshape(1, band))


def correlate_kernel(inverse, gathered, out, held, turn, bases, results, in_sem, out_sem):
    _, feed_groups, halves, owners, tall, some = held.shape
    depth = owners * tall

    def fetch(group):
        return pltpu.make_async_copy(gathered.at[:, :, :, group], held.at[group], in_sem.at[group])

    def store(slot, part):
        return pltpu.make_async_copy(results.at[slot, part], out.at[slot, part], out_sem.at[slot, part])

    fetch(0).start()
    source = lax.broadcasted_iota(jnp.int32, (depth, depth), 0)
    target = lax.broadcasted_iota(jnp.int32, (depth, depth), 1)
    imag = target // QUAD % 2
    turn[...] = jnp.where(
        source == target + QUAD - 2 * QUAD * imag, (2 * imag - 1).astype(jnp.float32), 0.0
    ).astype(jnp.bfloat16)
    lane = lax.broadcasted_iota(jnp.int32, (1, depth), 1)
    mine = lax.axis_index("feed")
    fetch(0).wait()
    for group in range(1, GROUPS):
        fetch(group).start()

    @pl.loop(0, GROUPS)
    def _(group):
        @pl.when(group > 0)
        def _():
            fetch(group).wait()

        own = jnp.concatenate([held[group, mine, half].reshape(depth, some).T for half in range(halves)], 0)
        bases[0] = own
        bases[1] = jnp.dot(own, turn[...], preferred_element_type=jnp.float32).astype(jnp.bfloat16)
        right = jnp.concatenate(
            [held[group, other, half].reshape(depth, some) for other in range(feed_groups) for half in range(halves)],
            1,
        )
        for index in range(QUAD):
            slot = group * QUAD + index
            mask = jnp.where(lane % QUAD == index, inverse, 0.0).astype(jnp.bfloat16)
            for part in range(2):
                results[slot, part] = jnp.dot(
                    bases[part] * mask, right, preferred_element_type=jnp.float32
                ).astype(jnp.bfloat16)
                store(slot, part).start()

    @pl.loop(0, CAP)
    def _(slot):
        for part in range(2):
            store(slot, part).wait()


def correlate(gathered):
    feed_groups, halves, owners, _, tall, some = gathered.shape
    depth, feeds = owners * tall, halves * some
    inverse = 1.0 / (depth // (2 * QUAD))
    shape = (CAP, 2, feeds, feed_groups * feeds)
    anywhere = pl.BlockSpec(memory_space=pl.ANY)
    return pl.pallas_call(
        functools.partial(correlate_kernel, inverse),
        out_shape=jax.ShapeDtypeStruct(shape, jnp.bfloat16),
        in_specs=[anywhere],
        out_specs=anywhere,
        scratch_shapes=[
            pltpu.VMEM((GROUPS, feed_groups, halves, owners, tall, some), jnp.bfloat16),
            pltpu.VMEM((depth, depth), jnp.bfloat16),
            pltpu.VMEM((2, feeds, depth), jnp.bfloat16),
            pltpu.VMEM(shape, jnp.bfloat16),
            pltpu.SemaphoreType.DMA((GROUPS,)),
            pltpu.SemaphoreType.DMA((CAP, 2)),
        ],
        compiler_params=pltpu.CompilerParams(vmem_limit_bytes=62 * MIB),
    )(gathered)


def solution(mesh):
    feed_groups, owners = mesh.shape["feed"], mesh.shape["freq"]

    def body(voltage, flags, owner_slot):
        return correlate(spread(voltage, flags, owner_slot, feed_groups, owners))

    placed = (P(None, "feed", "freq"), P("feed", None), P())
    return jax.shard_map(
        body, mesh=mesh, in_specs=placed, out_specs=P("freq", None, "feed", None), check_vma=False
    )
```

```python
import functools
import math

import jax
import jax.numpy as jnp
import ml_dtypes
import numpy as np
from jax import lax
from jax.experimental import pallas as pl
from jax.experimental.pallas import tpu as pltpu
from jax.sharding import PartitionSpec as P

CH = 1024
TAPS = 4
BAND_LO = 256
CAP = 20
QUAD = 4
GROUPS = CAP // QUAD
HALVES = 2
LOADS = 4
LAG = 3
WINDOW = 6
DEPTH = 2
MESH = pl.DeviceIdType.MESH
MIB = 1024 * 1024


def prototype():
    total = TAPS * CH
    position = np.arange(total, dtype=np.float64)
    taper = 0.5 - 0.5 * np.cos(2 * np.pi * (position + 0.5) / total)
    coeffs = np.sinc((position - total / 2 + 0.5) / CH) * taper
    coeffs = coeffs * np.sqrt(CH / np.sum(coeffs * coeffs))
    return coeffs.reshape(TAPS, CH).astype(np.float32)


def tables(band):
    phase = (np.arange(band)[:, None] + BAND_LO) * np.arange(CH)[None, :] % CH * (2 * np.pi / CH)
    cosine = np.cos(phase).astype(np.float32).astype(ml_dtypes.bfloat16)
    sine = np.sin(phase).astype(np.float32).astype(ml_dtypes.bfloat16)
    return np.concatenate([cosine, sine], 0)


def spread_kernel(
    count, owners, voltage, coeffs, table_hbm, flags, owner_slot, gathered,
    samples, table, slot_table, weighted, halo_out, halo_in, parts, outgoing,
    load_sem, table_sem, halo_send, halo_recv, local_sem,
    a_send, a_recv, x_send, x_recv, y_send, y_recv, d_send, d_recv,
):
    feed, me = lax.axis_index("feed"), lax.axis_index("freq")
    feeds = samples.shape[1] // HALVES
    band = flags.shape[1]
    rows = slot_table.shape[0]
    along_x, along_y = feed ^ 1, feed ^ 2
    halo = TAPS - 1

    barrier = pltpu.get_barrier_semaphore()
    for step in range(1, owners):
        pl.semaphore_signal(barrier, inc=1, device_id=(feed, me ^ step), device_id_type=MESH)
    for other in (along_x, along_y):
        pl.semaphore_signal(barrier, inc=1, device_id=(other, me), device_id_type=MESH)

    tables_in = pltpu.make_async_copy(table_hbm, table, table_sem)
    tables_in.start()
    share = samples.shape[1] // LOADS

    def load(index):
        here = slice(index * share, (index + 1) * share)
        return pltpu.make_async_copy(voltage.at[:, here, :], samples.at[:, here, :], load_sem.at[index])

    for index in range(LOADS):
        load(index).start()

    row = lax.broadcasted_iota(jnp.int32, (rows, band), 0)
    slot = row // (2 * QUAD) * QUAD + row % QUAD
    kept = jnp.where(slot == owner_slot[...], flags[...].astype(jnp.float32), 0.0)
    kept = kept * (1.0 / math.sqrt(CH))
    imag_row = row // QUAD % 2 == 1
    real_kept = jnp.where(imag_row, 0.0, kept)
    imag_kept = jnp.where(imag_row, kept, 0.0)
    tables_in.wait()
    for part, pick in enumerate(([real_kept, -imag_kept], [imag_kept, real_kept])):
        slot_table[:, part * CH : (part + 1) * CH] = jnp.dot(
            jnp.concatenate(pick, 1).astype(jnp.bfloat16), table[...], preferred_element_type=jnp.float32
        ).astype(jnp.bfloat16)

    ahead = [
        [(tap, spectrum + tap - count) for tap in range(TAPS) if 0 <= spectrum + tap - count < count]
        for spectrum in range(count - halo, count)
    ]
    within = [[(tap, spectrum + tap) for tap in range(TAPS) if spectrum + tap < count] for spectrum in range(count)]

    def weigh(half, sums):
        tall = 32
        for index in range(half * LOADS // HALVES, (half + 1) * LOADS // HALVES):
            if sums is ahead:
                load(index).wait()

            @pl.loop(0, share // tall)
            def _(step):
                first = pl.multiple_of(index * share + step * tall, tall)
                placed = first - half * feeds
                for part in range(2):
                    for lane in range(0, CH, 128):
                        blocks = [
                            samples[
                                part, pl.ds(first, tall), block * CH + lane : block * CH + lane + 128
                            ].astype(jnp.float32)
                            for block in range(count)
                        ]
                        for place, pairs in enumerate(sums):
                            total = None
                            for tap, block in pairs:
                                term = blocks[block] * coeffs[tap : tap + 1, lane : lane + 128]
                                total = term if total is None else total + term
                            weighted[
                                pl.ds(pl.multiple_of(place * feeds + placed, tall), tall),
                                part * CH + lane : part * CH + lane + 128,
                            ] = total.astype(jnp.bfloat16)

    def transform(places):
        return lax.dot_general(
            slot_table[...],
            weighted[0 : places * feeds, :],
            (((1,), (1,)), ((), ())),
            preferred_element_type=jnp.float32,
        )

    def backward(half):
        return pltpu.make_async_remote_copy(
            src_ref=halo_out.at[half],
            dst_ref=halo_in.at[half],
            send_sem=halo_send.at[half],
            recv_sem=halo_recv.at[half],
            device_id=(feed, jnp.maximum(me - 1, 0)),
            device_id_type=MESH,
        )

    def send_halo(half):
        halo_out[half] = transform(halo).astype(jnp.bfloat16)
        if half == 0:
            pl.semaphore_wait(barrier, owners + 1)

        @pl.when(me > 0)
        def _():
            backward(half).start()

    def transform_own():
        parts[...] = transform(count)

    def finish(half):
        @pl.when(me < owners - 1)
        def _():
            backward(half).wait_recv()
            parts[:, (count - halo) * feeds :] += halo_in[half].astype(jnp.float32)

        for place in range(0, count, 2):
            pair = [
                parts[:, (place + k) * feeds : (place + k + 1) * feeds].reshape(rows // 8, 8, feeds)
                for k in range(2)
            ]
            outgoing[half, :, place * 8 : place * 8 + 16, :] = jnp.concatenate(pair, 1).astype(jnp.bfloat16)

    def chunk(half, owner):
        return outgoing.at[half, pl.ds(owner * GROUPS, GROUPS)]

    def remote(source, target, send, recv, device):
        return pltpu.make_async_remote_copy(
            src_ref=source, dst_ref=target, send_sem=send, recv_sem=recv, device_id=device, device_id_type=MESH
        )

    def keep(half):
        return pltpu.make_async_copy(chunk(half, me), gathered.at[feed, half, me], local_sem.at[half])

    def to_owner(half, t):
        return remote(
            chunk(half, me ^ t), gathered.at[feed, half, me],
            a_send.at[half, t], a_recv.at[half, t], (feed, me ^ t),
        )

    def shared(half, t):
        return chunk(half, me) if t == 0 else gathered.at[feed, half, me ^ t]

    def to_x(half, t):
        return remote(
            shared(half, t), gathered.at[feed, half, me ^ t],
            x_send.at[half, t], x_recv.at[half, t], (along_x, me),
        )

    def to_y(half, t):
        return remote(
            shared(half, t), gathered.at[feed, half, me ^ t],
            y_send.at[half, t], y_recv.at[half, t], (along_y, me),
        )

    def onward(half, t):
        origin, target = (along_x, along_y) if t % 2 else (along_y, along_x)
        block = gathered.at[origin, half, me ^ t]
        return remote(block, block, d_send.at[half, t], d_recv.at[half, t], (target, me))

    def pass_on(half, t):
        (to_x if t % 2 else to_y)(half, t).wait_recv()
        onward(half, t).start()

    steps = sorted(
        [(half, t) for half in range(HALVES) for t in range(owners)],
        key=lambda step: (step[1] + LAG * step[0], -step[0]),
    )
    early = [(0, t) for t in range(min(LAG + 1, owners))] if HALVES > 1 else []
    steps = early + [step for step in steps if step not in early]
    leaving = [step for step in steps if step[1]]
    handled = []

    def leave(half, limit):
        ready = [step for step in leaving if step[0] <= half][:limit]
        for step in ready:
            leaving.remove(step)
            to_owner(*step).start()

    def handle(step, ready):
        half, t = step
        if t:
            assert step not in leaving
            to_owner(half, t).wait_recv()
            leave(ready, 1)
        to_x(half, t).start()
        to_y(half, t).start()
        handled.append(step)
        if len(handled) > DEPTH:
            pass_on(*handled[-1 - DEPTH])

    weigh(0, ahead)
    send_halo(0)
    weigh(0, within)
    transform_own()
    if HALVES > 1:
        weigh(1, ahead)
        send_halo(1)
    finish(0)
    keep(0).start()
    handle((0, 0), 0)
    leave(0, WINDOW)
    if HALVES > 1:
        weigh(1, within)
        handle(early[1], 0)
        transform_own()
        for step in early[2:]:
            handle(step, 0)
        finish(1)
        keep(1).start()
        handle((1, 0), 1)
        leave(1, WINDOW)
    for step in steps:
        if step not in handled:
            handle(step, HALVES - 1)
    for step in handled[-DEPTH:]:
        pass_on(*step)

    for half, t in steps:
        (to_y if t % 2 else to_x)(half, t).wait_recv()
        onward(half, t).wait_recv()
        if t:
            to_owner(half, t).wait_send()
        to_x(half, t).wait_send()
        to_y(half, t).wait_send()
        onward(half, t).wait_send()
    for half in range(HALVES):
        keep(half).wait()

        @pl.when(me > 0)
        def _():
            backward(half).wait_send()


def spread(voltage, flags, owner_slot, feed_groups, owners):
    feeds, samples = voltage.shape[1:]
    feeds = feeds // HALVES
    band = flags.shape[1]
    count = samples // CH
    rows = owners * CAP * 2
    tall = count * 2 * QUAD
    vmem, anywhere = pl.BlockSpec(memory_space=pltpu.VMEM), pl.BlockSpec(memory_space=pl.ANY)
    dma = pltpu.SemaphoreType.DMA
    return pl.pallas_call(
        functools.partial(spread_kernel, count, owners),
        out_shape=jax.ShapeDtypeStruct(
            (feed_groups, HALVES, owners, GROUPS, tall, feeds), jnp.bfloat16
        ),
        in_specs=[anywhere, vmem, anywhere, vmem, vmem],
        out_specs=anywhere,
        scratch_shapes=[
            pltpu.VMEM((2, HALVES * feeds, samples), jnp.bfloat16),
            pltpu.VMEM((2 * band, CH), jnp.bfloat16),
            pltpu.VMEM((rows, 2 * CH), jnp.bfloat16),
            pltpu.VMEM((count * feeds, 2 * CH), jnp.bfloat16),
            pltpu.VMEM((HALVES, rows, (TAPS - 1) * feeds), jnp.bfloat16),
            pltpu.VMEM((HALVES, rows, (TAPS - 1) * feeds), jnp.bfloat16),
            pltpu.VMEM((rows, count * feeds), jnp.float32),
            pltpu.VMEM((HALVES, owners * GROUPS, tall, feeds), jnp.bfloat16),
        ]
        + [dma((LOADS,)), dma]
        + [dma((HALVES,))] * 3
        + [dma((HALVES, owners))] * 8,
        compiler_params=pltpu.CompilerParams(
            collective_id=0, has_side_effects=True, vmem_limit_bytes=62 * MIB
        ),
    )(voltage, prototype(), tables(band), flags, owner_slot.reshape(1, band))


def correlate_kernel(inverse, gathered, out, held, turn, bases, results, in_sem, out_sem):
    _, feed_groups, halves, owners, tall, some = held.shape
    depth = owners * tall

    def fetch(group):
        return pltpu.make_async_copy(gathered.at[:, :, :, group], held.at[group], in_sem.at[group])

    def store(slot, part):
        return pltpu.make_async_copy(results.at[slot, part], out.at[slot, part], out_sem.at[slot, part])

    fetch(0).start()
    source = lax.broadcasted_iota(jnp.int32, (depth, depth), 0)
    target = lax.broadcasted_iota(jnp.int32, (depth, depth), 1)
    imag = target // QUAD % 2
    turn[...] = jnp.where(
        source == target + QUAD - 2 * QUAD * imag, (2 * imag - 1).astype(jnp.float32), 0.0
    ).astype(jnp.bfloat16)
    lane = lax.broadcasted_iota(jnp.int32, (1, depth), 1)
    mine = lax.axis_index("feed")
    fetch(0).wait()
    for group in range(1, GROUPS):
        fetch(group).start()

    @pl.loop(0, GROUPS)
    def _(group):
        @pl.when(group > 0)
        def _():
            fetch(group).wait()

        own = jnp.concatenate([held[group, mine, half].reshape(depth, some).T for half in range(halves)], 0)
        bases[0] = own
        bases[1] = jnp.dot(own, turn[...], preferred_element_type=jnp.float32).astype(jnp.bfloat16)
        right = jnp.concatenate(
            [held[group, other, half].reshape(depth, some) for other in range(feed_groups) for half in range(halves)],
            1,
        )
        for index in range(QUAD):
            slot = group * QUAD + index
            mask = jnp.where(lane % QUAD == index, inverse, 0.0).astype(jnp.bfloat16)
            for part in range(2):
                results[slot, part] = jnp.dot(
                    bases[part] * mask, right, preferred_element_type=jnp.float32
                ).astype(jnp.bfloat16)
                store(slot, part).start()

    @pl.loop(0, CAP)
    def _(slot):
        for part in range(2):
            store(slot, part).wait()


def correlate(gathered):
    feed_groups, halves, owners, _, tall, some = gathered.shape
    depth, feeds = owners * tall, halves * some
    inverse = 1.0 / (depth // (2 * QUAD))
    shape = (CAP, 2, feeds, feed_groups * feeds)
    anywhere = pl.BlockSpec(memory_space=pl.ANY)
    return pl.pallas_call(
        functools.partial(correlate_kernel, inverse),
        out_shape=jax.ShapeDtypeStruct(shape, jnp.bfloat16),
        in_specs=[anywhere],
        out_specs=anywhere,
        scratch_shapes=[
            pltpu.VMEM((GROUPS, feed_groups, halves, owners, tall, some), jnp.bfloat16),
            pltpu.VMEM((depth, depth), jnp.bfloat16),
            pltpu.VMEM((2, feeds, depth), jnp.bfloat16),
            pltpu.VMEM(shape, jnp.bfloat16),
            pltpu.SemaphoreType.DMA((GROUPS,)),
            pltpu.SemaphoreType.DMA((CAP, 2)),
        ],
        compiler_params=pltpu.CompilerParams(vmem_limit_bytes=62 * MIB),
    )(gathered)


def solution(mesh):
    feed_groups, owners = mesh.shape["feed"], mesh.shape["freq"]

    def body(voltage, flags, owner_slot):
        return correlate(spread(voltage, flags, owner_slot, feed_groups, owners))

    placed = (P(None, "feed", "freq"), P("feed", None), P())
    return jax.shard_map(
        body, mesh=mesh, in_specs=placed, out_specs=P("freq", None, "feed", None), check_vma=False
    )
```
